512 devices in a mesh: half: 2 (over core), row: 16 (over z), col: 16 (over y, x).
Axes of the slice: x: 4, y: 4, z: 16, core: 2. Of those that a mesh axis runs over, the one named last changes fastest.
Arguments:
- child_front: float32 [2, 8192, 8192], P('half', 'row', 'col'), as said below
- child_map: int32 [2, 48], P('half'), may hold values from 0 to 63, as said below
- root_front: float32 [8192, 16, 2, 256], P('row', 'col', 'half'), as said below
Outputs:
- child_panel: float32 [2, 512, 8192], P('half', None, 'col')
- root_panel: float32 [512, 16, 2, 256], P(None, 'col', 'half')
- root_update: float32 [8192, 16, 2, 256], P('row', 'col', 'half')
The draws below stay inside these ranges and needn't reach their ends.
Inputs may be any that keep to these rules, and one draw needn't show every extreme that they name: `child_map`: for child h, the update blocks of row part k (the 3 blocks after that part's first block) map in increasing order to distinct blocks among the root's blocks k * 4 to (k + 1) * 4 - 1. `child_front`: each child's front is symmetric and positive definite. `root_front`: the root front is symmetric and positive definite.
All inputs are finite; a program needn't handle non-finite values.
Results may differ from the reference program's by a relative error of at most 0.0001.
Values sent between devices are 32-bit elements; how exact they have to be, the bound alone decides.
A program may use at most 64 MiB of HBM per device.

```python
import jax
import jax.numpy as jnp
from jax import lax

BLK = 128
PB = 32
F = 8192
R = 8192
N_ROW = 16
N_COL = 16


def gram_matrix(draw_key, matrix_order, inner_width, scales):
    factor = jax.random.normal(draw_key, (matrix_order, inner_width), jnp.float32)
    square = jnp.dot(factor, factor.T, precision=lax.Precision.HIGHEST) / inner_width
    square = 0.5 * (square + square.T)
    return square + 0.5 * jnp.diag(scales)


def draw_child_front(key, part):
    key = jax.random.fold_in(key, 1)
    subkeys = jax.random.split(key, 2)
    scales = jnp.ones((2, F), jnp.float32)
    return jnp.stack([gram_matrix(subkeys[0], F, F // 4, scales[0]), gram_matrix(subkeys[1], F, F // 4, scales[1])])


def draw_root_front(key, part):
    key = jax.random.fold_in(key, 2)
    subkeys = jax.random.split(key, 1)
    scales = jnp.ones((R,), jnp.float32)
    square = gram_matrix(subkeys[0], R, R // 4, scales)
    return square.reshape(R, N_COL, 2, R // (2 * N_COL))


def draw_child_map(key, part):
    key = jax.random.fold_in(key, 3)
    per_part = F // (BLK * N_ROW) - 1
    root_tiles = R // (BLK * N_ROW)
    scores = jax.random.randint(key, (2, N_ROW, root_tiles), 0, 1 << 20) * root_tiles + jnp.arange(root_tiles, dtype=jnp.int32)
    chosen = jnp.sort(lax.top_k(scores, per_part)[1], axis=-1)
    chosen = chosen + jnp.arange(N_ROW, dtype=jnp.int32)[None, :, None] * root_tiles
    return chosen.reshape(2, N_ROW * per_part).astype(jnp.int32)


def setup_inputs(seed: int = 0) -> dict:
    key_of = jax.random.split(jax.random.key(seed), 4)
    child_front = draw_child_front(jax.random.fold_in(key_of[3], 71), 0)
    child_map = draw_child_map(jax.random.fold_in(key_of[3], 71), 0)
    root_front = draw_root_front(jax.random.fold_in(key_of[3], 71), 0)
    return dict(child_front=child_front, child_map=child_map, root_front=root_front)


def lower_solve(factor, right):
    return lax.linalg.triangular_solve(factor, right, left_side=True, lower=True)

def pivot_rows(part_rows):
    within = jnp.arange(PB, dtype=jnp.int32)
    starts = jnp.arange(N_ROW, dtype=jnp.int32) * part_rows
    return (starts[:, None] + within[None, :]).reshape(-1)

def partial_factor(matrix, pivots):
    strips = matrix[pivots, :]
    factor = jnp.linalg.cholesky(strips[:, pivots])
    panel = lower_solve(factor, strips)
    update = matrix - jnp.dot(panel.T.astype(jnp.float32), panel.astype(jnp.float32), precision=lax.Precision.HIGHEST, preferred_element_type=jnp.float32)
    return (panel, update)

def spread_update(update, targets):
    per_part = F // (BLK * N_ROW) - 1
    which = jnp.arange(N_ROW * per_part, dtype=jnp.int32)
    child_tile = which // per_part * (per_part + 1) + 1 + which % per_part
    within = jnp.arange(BLK, dtype=jnp.int32)
    child_rows = (child_tile[:, None] * BLK + within[None, :]).reshape(-1)
    root_rows = (targets.astype(jnp.int32)[:, None] * BLK + within[None, :]).reshape(-1)
    picked = update[child_rows, :][:, child_rows]
    by_rows = jnp.zeros((R, picked.shape[1]), jnp.float32).at[root_rows, :].add(picked)
    return jnp.zeros((R, R), jnp.float32).at[:, root_rows].add(by_rows)

def reference(child_front, child_map, root_front):
    child_pivots = pivot_rows(F // N_ROW)
    panels = []
    spreads = []
    for which in range(2):
        panel, update = partial_factor(child_front[which], child_pivots)
        panels.append(panel)
        spreads.append(spread_update(update, child_map[which]))
    assembled = root_front.reshape(R, R) + (spreads[0] + spreads[1])
    root_panel, root_update = partial_factor(assembled, pivot_rows(R // N_ROW))
    width = R // (2 * N_COL)
    return (jnp.stack(panels), root_panel.reshape(root_panel.shape[0], N_COL, 2, width), root_update.reshape(R, N_COL, 2, width))
```

```python
import functools

import jax
import jax.numpy as jnp
from jax import lax
from jax.experimental import pallas as pl
from jax.experimental.pallas import tpu as pltpu
from jax.sharding import PartitionSpec as P

N = 16
PB = 32
BLK = 128
ORD = N * PB
F32 = jnp.float32
MESH = pl.DeviceIdType.MESH
VM = pl.BlockSpec(memory_space=pltpu.VMEM)
SM = pl.BlockSpec(memory_space=pltpu.SMEM)


def dot(a, b):
    return lax.dot_general(
        a, b, (((1,), (0,)), ((), ())), precision=lax.Precision.HIGHEST, preferred_element_type=F32
    )


def dot_t(a, b):
    return lax.dot_general(
        a, b, (((0,), (0,)), ((), ())), precision=lax.Precision.HIGHEST, preferred_element_type=F32
    )


def factor_tile(a, at_half):
    n, full = BLK // 8, (8, BLK)
    lane = lax.broadcasted_iota(jnp.int32, full, 1)
    sub = lax.broadcasted_iota(jnp.int32, full, 0)
    rows = [a[8 * i : 8 * i + 8] for i in range(n)]
    inv = [jnp.where(lane == sub + 8 * i, 1.0, 0.0).astype(F32) for i in range(n)]
    out = []
    for m in range(n):
        if m == n // 2:
            at_half()
        j0 = 8 * m
        top, eye = rows[m], inv[m]
        cols = [jnp.broadcast_to(top[:, j0 + k : j0 + k + 1], full) for k in range(8)]
        e = {(i, k): jnp.broadcast_to(cols[k][i : i + 1], full) for k in range(8) for i in range(k, 8)}
        u = [jnp.broadcast_to(top[i : i + 1], full) for i in range(8)]
        x = [jnp.broadcast_to(eye[i : i + 1], full) for i in range(8)]
        r, low = [None] * 8, {}
        for k in range(8):
            r[k] = lax.rsqrt(e[k, k])
            for i in range(k + 1, 8):
                low[i, k] = e[i, k] * r[k]
            for i in range(k + 1, 8):
                for j in range(k + 1, i + 1):
                    e[i, j] = e[i, j] - low[i, k] * low[j, k]
            u[k] = u[k] * r[k]
            x[k] = x[k] * r[k]
            for i in range(k + 1, 8):
                u[i] = u[i] - low[i, k] * u[k]
                x[i] = x[i] - low[i, k] * x[k]
        done = x[0]
        for k in range(1, 8):
            done = jnp.where(sub == k, x[k], done)
        out.append(done)
        for q in range(m + 1, n):
            src = rows[q]
            t, w, lq = src, inv[q], []
            for k in range(8):
                v = jnp.broadcast_to(src[:, j0 + k : j0 + k + 1], full)
                for p in range(k):
                    v = v - lq[p] * low[k, p]
                v = v * r[k]
                lq.append(v)
                t = t - v * u[k]
                w = w - v * x[k]
            rows[q], inv[q] = t, w
    return jnp.concatenate(out, axis=0)


def factor(a_ref, i_ref, relay):
    def step(j, carry):
        relay(2 * j + 1)
        jb = pl.multiple_of(j * BLK, BLK)
        inv = factor_tile(a_ref[pl.ds(jb, BLK), pl.ds(jb, BLK)], lambda: relay(2 * j + 2))
        i_ref[j] = inv
        a_ref[pl.ds(jb, BLK), :] = dot(inv, a_ref[pl.ds(jb, BLK), :])
        for i in range(1, ORD // BLK):

            @pl.when(i > j)
            def _(i=i):
                here = slice(BLK * i, BLK * i + BLK)
                a_ref[here, :] -= dot_t(a_ref[pl.ds(jb, BLK), here], a_ref[pl.ds(jb, BLK), :])

        return carry

    lax.fori_loop(0, ORD // BLK, step, 0)


def solve(a_ref, i_ref, s_ref, y_ref):
    for j in range(ORD // BLK):
        here = slice(BLK * j, BLK * j + BLK)
        acc = s_ref[here, :]
        if j:
            acc = acc - dot_t(a_ref[0 : BLK * j, here], y_ref[0 : BLK * j, :])
        y_ref[here, :] = dot(i_ref[j], acc)


def remote(src, dst, sends, recvs, k, dev):
    return pltpu.make_async_remote_copy(
        src_ref=src,
        dst_ref=dst,
        send_sem=sends.at[k],
        recv_sem=recvs.at[k],
        device_id=dev,
        device_id_type=MESH,
    )


def each(lo, hi, fn):
    def go(k, carry):
        fn(k)
        return carry

    lax.fori_loop(lo, hi, go, 0)


def rows_of(k):
    return pl.ds(pl.multiple_of(k * PB, PB), PB)


def ring(ref, row, sems):
    rs, rr, ls, lr = sems
    right, left = lax.rem(row + 1, N), lax.rem(row + N - 1, N)

    def to_right(s):
        view = ref.at[rows_of(lax.rem(row - s + N, N)), :]
        return remote(view, view, rs, rr, s, {"row": right})

    def to_left(s):
        view = ref.at[rows_of(lax.rem(row + s, N)), :]
        return remote(view, view, ls, lr, s, {"row": left})

    def got_right(s):
        view = ref.at[rows_of(lax.rem(row - 1 - s + 2 * N, N)), :]
        return remote(view, view, rs, rr, s, {"row": right})

    def got_left(s):
        view = ref.at[rows_of(lax.rem(row + 1 + s, N)), :]
        return remote(view, view, ls, lr, s, {"row": left})

    def start():
        to_right(0).start()
        to_left(0).start()

    def relay(s):
        @pl.when(s < 8)
        def _():
            got_right(s - 1).wait_recv()
            to_right(s).start()

        @pl.when(s < 7)
        def _():
            got_left(s - 1).wait_recv()
            to_left(s).start()

    def finish():
        got_right(7).wait_recv()
        got_left(6).wait_recv()
        each(0, 8, lambda s: to_right(s).wait_send())
        each(0, 7, lambda s: to_left(s).wait_send())

    return start, relay, finish


def packed_piece(tile):
    turned = jnp.transpose(tile)
    lane = lax.broadcasted_iota(jnp.int32, (8, BLK), 1)
    out = turned[0:8]
    for g in range(1, 4):
        out = jnp.where(lane >= PB * g, pltpu.roll(turned[8 * g : 8 * g + 8], PB * g, 1), out)
    return out


def unpack_pieces(pc_ref, rb_ref):
    lane = lax.broadcasted_iota(jnp.int32, (8, BLK), 1)
    for l in range(4):
        pcs = [pc_ref[4 * l + kk] for kk in range(4)]
        for g in range(4):
            out = None
            for kk in range(4):
                shift = (PB * (kk - g)) % BLK
                v = pltpu.roll(pcs[kk], shift, 1) if shift else pcs[kk]
                out = v if kk == 0 else jnp.where(lane >= PB * kk, v, out)
            rb_ref[8 * g : 8 * g + 8, BLK * l : BLK * l + BLK] = out


def greet(devices):
    barrier = pltpu.get_barrier_semaphore()
    total = 0
    for count, dev in devices:
        each(1, count + 1, lambda k, dev=dev: pl.semaphore_signal(barrier, inc=1, device_id=dev(k), device_id_type=MESH))
        total += count
    pl.semaphore_wait(barrier, total)


def child_kernel(
    map_ref, blk_ref, root_ref, panel_ref, asm_ref,
    pc, rb, a_ref, inv_ref, sc, sr, yr, upd, give, take,
    s1, r1, s2, r2, s3, r3, rs, rr, ls, lr, xs, xr,
):
    half, row, col = lax.axis_index("half"), lax.axis_index("row"), lax.axis_index("col")

    def row_peer(k):
        return {"row": lax.rem(row + k, N)}

    def col_peer(k):
        return {"col": lax.rem(col + k, N)}

    other = {"half": 1 - half}
    piece = packed_piece(blk_ref[0:BLK, 0:BLK])
    pc[row] = piece
    greet([(N - 1, row_peer), (N - 1, col_peer), (1, lambda k: other)])

    def piece_to(k):
        return remote(pc.at[row], pc.at[row], s1, r1, k, row_peer(k))

    def piece_from(k):
        view = pc.at[lax.rem(row - k + N, N)]
        return remote(view, view, s1, r1, k, row_peer(k))

    each(1, N, lambda k: piece_to(k).start())
    sc[rows_of(row), :] = blk_ref[0:PB, :]
    mine = jnp.concatenate([jnp.transpose(blk_ref[BLK * i : BLK * i + BLK, 0:BLK])[0:PB] for i in range(1, 4)], axis=1)
    sr[rows_of(col), :] = mine
    each(1, N, lambda k: piece_from(k).wait_recv())
    unpack_pieces(pc, rb)
    a_ref[rows_of(col), :] = rb[...]

    def block_to(k):
        return remote(rb, a_ref.at[rows_of(col), :], s2, r2, k, col_peer(k))

    def block_from(k):
        return remote(rb, a_ref.at[rows_of(lax.rem(col - k + N, N)), :], s2, r2, k, col_peer(k))

    each(1, N, lambda k: block_to(k).start())
    start, relay, finish = ring(sc, row, (rs, rr, ls, lr))
    start()
    each(1, N, lambda k: block_from(k).wait_recv())

    def column_to(k):
        view = sr.at[rows_of(col), :]
        return remote(view, view, s3, r3, k, col_peer(k))

    def column_from(k):
        view = sr.at[rows_of(lax.rem(col - k + N, N)), :]
        return remote(view, view, s3, r3, k, col_peer(k))

    each(1, N, lambda k: column_to(k).start())
    factor(a_ref, inv_ref, relay)
    finish()
    each(1, N, lambda k: column_from(k).wait_recv())
    solve(a_ref, inv_ref, sc, panel_ref)
    solve(a_ref, inv_ref, sr, yr)
    for u in range(3):
        rows = slice(BLK * u, BLK * u + BLK)
        block = blk_ref[BLK + BLK * u : 2 * BLK + BLK * u, BLK:] - dot_t(yr[:, rows], panel_ref[:, BLK:])
        for v in range(3):
            upd[3 * u + v] = block[:, BLK * v : BLK * v + BLK]

    def source(part, target):
        found = jnp.int32(-1)
        for u in range(3):
            found = jnp.where(map_ref[0, 3 * part + u] == 4 * part + target, jnp.int32(u), found)
        return found

    def tile(p, q):
        value = upd[jnp.maximum(p, 0) * 3 + jnp.maximum(q, 0)]
        return jnp.where(jnp.logical_and(p >= 0, q >= 0), value, 0.0)

    from_rows = [source(row, a) for a in range(4)]
    theirs = [source(col, 2 * (1 - half) + b) for b in range(2)]
    ours = [source(col, 2 * half + b) for b in range(2)]
    for a in range(4):
        for b in range(2):
            give[BLK * a : BLK * a + BLK, BLK * b : BLK * b + BLK] = tile(from_rows[a], theirs[b])
    swap = remote(give, take, xs, xr, 0, other)
    swap.start()
    for a in range(4):
        for b in range(2):
            at = (slice(BLK * a, BLK * a + BLK), slice(BLK * b, BLK * b + BLK))
            asm_ref[at] = root_ref[at] + tile(from_rows[a], ours[b])
    swap.wait_recv()
    asm_ref[...] += take[...]
    swap.wait_send()
    each(1, N, lambda k: piece_to(k).wait_send())
    each(1, N, lambda k: block_to(k).wait_send())
    each(1, N, lambda k: column_to(k).wait_send())


def root_kernel(
    asm_ref, panel_ref, out_ref,
    pc, rb, a_ref, inv_ref, sc, sr, yr,
    s1, r1, s2, r2, s3, r3, s4, r4, rs, rr, ls, lr,
):
    half, row, col = lax.axis_index("half"), lax.axis_index("row"), lax.axis_index("col")
    dma = functools.partial(remote)

    def row_peer(k):
        return {"half": lax.rem(half + k // N, 2), "row": lax.rem(row + lax.rem(k, N), N)}

    def col_peer(k):
        return {"half": lax.rem(half + k // N, 2), "col": lax.rem(col + lax.rem(k, N), N)}

    pc[row] = packed_piece(asm_ref[0:BLK, 0:BLK])
    greet([(2 * N - 1, row_peer), (N - 1, col_peer), (N - 1, lambda k: col_peer(k + N))])

    def piece_to(k):
        return dma(pc.at[row], pc.at[row], s1, r1, k, row_peer(k))

    def piece_from(k):
        view = pc.at[lax.rem(row - lax.rem(k, N) + N, N)]
        return dma(view, view, s1, r1, k, row_peer(k))

    @pl.when(half == 0)
    def _():
        each(1, 2 * N, lambda k: piece_to(k).start())

    sc[rows_of(row), :] = asm_ref[0:PB, :]

    @pl.when(half == 0)
    def _():
        sr[rows_of(col), :] = jnp.concatenate(
            [jnp.transpose(asm_ref[BLK * i : BLK * i + BLK, 0:BLK])[0:PB] for i in range(4)], axis=1
        )
        each(1, N, lambda k: piece_from(k).wait_recv())

    @pl.when(half == 1)
    def _():
        each(N, 2 * N, lambda k: piece_from(k).wait_recv())

    unpack_pieces(pc, rb)
    a_ref[rows_of(col), :] = rb[...]

    def part(c):
        return pl.ds(pl.multiple_of(c * PB + half * 16, 16), 16)

    def other_part(c):
        return pl.ds(pl.multiple_of(c * PB + (1 - half) * 16, 16), 16)

    own_rows = pl.ds(pl.multiple_of(half * 16, 16), 16)

    def block_to(k):
        return dma(rb.at[own_rows, :], a_ref.at[part(col), :], s2, r2, k, col_peer(k))

    def block_from(k):
        view = a_ref.at[part(lax.rem(col - k + N, N)), :]
        return dma(view, view, s2, r2, k, col_peer(k))

    def pass_on(k):
        view = a_ref.at[part(lax.rem(col - k + N, N)), :]
        return dma(view, view, s4, r4, k, {"half": 1 - half})

    def passed(k):
        view = a_ref.at[other_part(lax.rem(col - k + N, N)), :]
        return dma(view, view, s4, r4, k, {"half": 1 - half})

    each(1, N, lambda k: block_to(k).start())
    start, relay, finish = ring(sc, row, (rs, rr, ls, lr))
    start()

    def forward(k):
        block_from(k).wait_recv()
        pass_on(k).start()

    each(1, N, forward)

    def column_to(k):
        view = sr.at[rows_of(col), :]
        return dma(view, view, s3, r3, k, col_peer(k))

    def column_from(k):
        view = sr.at[rows_of(lax.rem(col - lax.rem(k, N) + N, N)), :]
        return dma(view, view, s3, r3, k, col_peer(k))

    @pl.when(half == 0)
    def _():
        each(1, 2 * N, lambda k: column_to(k).start())

    each(1, N, lambda k: passed(k).wait_recv())
    each(1, N, lambda k: pass_on(k).wait_send())
    factor(a_ref, inv_ref, relay)
    finish()

    @pl.when(half == 0)
    def _():
        each(1, N, lambda k: column_from(k).wait_recv())

    @pl.when(half == 1)
    def _():
        each(N, 2 * N, lambda k: column_from(k).wait_recv())

    solve(a_ref, inv_ref, sc, panel_ref)
    solve(a_ref, inv_ref, sr, yr)
    for i in range(4):
        rows = slice(BLK * i, BLK * i + BLK)
        out_ref[rows, :] = asm_ref[rows, :] - dot_t(yr[:, rows], panel_ref[...])
    each(1, N, lambda k: block_to(k).wait_send())

    @pl.when(half == 0)
    def _():
        each(1, 2 * N, lambda k: piece_to(k).wait_send())
        each(1, 2 * N, lambda k: column_to(k).wait_send())


def sems(*sizes):
    return [pltpu.SemaphoreType.DMA((n,)) for n in sizes]


def body(child_front, child_map, root_front):
    root = root_front.reshape(ORD, ORD // 2)
    sds = jax.ShapeDtypeStruct
    panel, asm = pl.pallas_call(
        child_kernel,
        out_shape=[sds((ORD, ORD), F32), sds((ORD, ORD // 2), F32)],
        in_specs=[SM, VM, VM],
        out_specs=[VM, VM],
        scratch_shapes=[
            pltpu.VMEM((N, 8, BLK), F32),
            pltpu.VMEM((PB, ORD), F32),
            pltpu.VMEM((ORD, ORD), F32),
            pltpu.VMEM((4, BLK, BLK), F32),
            pltpu.VMEM((ORD, ORD), F32),
            pltpu.VMEM((ORD, 3 * BLK), F32),
            pltpu.VMEM((ORD, 3 * BLK), F32),
            pltpu.VMEM((9, BLK, BLK), F32),
            pltpu.VMEM((ORD, ORD // 2), F32),
            pltpu.VMEM((ORD, ORD // 2), F32),
            *sems(N, N, N, N, N, N, 8, 8, 8, 8, 1, 1),
        ],
        compiler_params=pltpu.CompilerParams(
            collective_id=0, has_side_effects=True, vmem_limit_bytes=40 * 2**20
        ),
    )(child_map, child_front[0], root)
    root_panel, root_update = pl.pallas_call(
        root_kernel,
        out_shape=[sds((ORD, ORD // 2), F32), sds((ORD, ORD // 2), F32)],
        in_specs=[VM],
        out_specs=[VM, VM],
        scratch_shapes=[
            pltpu.VMEM((N, 8, BLK), F32),
            pltpu.VMEM((PB, ORD), F32),
            pltpu.VMEM((ORD, ORD), F32),
            pltpu.VMEM((4, BLK, BLK), F32),
            pltpu.VMEM((ORD, ORD // 2), F32),
            pltpu.VMEM((ORD, ORD), F32),
            pltpu.VMEM((ORD, ORD), F32),
            *sems(2 * N, 2 * N, N, N, 2 * N, 2 * N, N, N, 8, 8, 8, 8),
        ],
        compiler_params=pltpu.CompilerParams(
            collective_id=1, has_side_effects=True, vmem_limit_bytes=40 * 2**20
        ),
    )(asm)
    return (panel[None], root_panel[:, None, None, :], root_update[:, None, None, :])


def solution(mesh):
    return jax.shard_map(
        body,
        mesh=mesh,
        in_specs=(P("half", "row", "col"), P("half", None), P("row", "col", "half", None)),
        out_specs=(
            P("half", None, "col"),
            P(None, "col", "half", None),
            P("row", "col", "half", None),
        ),
        check_vma=False,
    )
```

```python
import jax
import jax.numpy as jnp
from jax import lax
from jax.experimental import pallas as pl
from jax.experimental.pallas import tpu as pltpu
from jax.sharding import PartitionSpec as P

N = 16
PB = 32
BLK = 128
ORD = N * PB
F32 = jnp.float32
MESH = pl.DeviceIdType.MESH
VM = pl.BlockSpec(memory_space=pltpu.VMEM)
SM = pl.BlockSpec(memory_space=pltpu.SMEM)


def dot(a, b):
    return lax.dot_general(
        a, b, (((1,), (0,)), ((), ())), precision=lax.Precision.HIGHEST, preferred_element_type=F32
    )


def dot_t(a, b):
    return lax.dot_general(
        a, b, (((0,), (0,)), ((), ())), precision=lax.Precision.HIGHEST, preferred_element_type=F32
    )


def factor_tile(a, at_half):
    n, full = BLK // 8, (8, BLK)
    lane = lax.broadcasted_iota(jnp.int32, full, 1)
    sub = lax.broadcasted_iota(jnp.int32, full, 0)
    rows = [a[8 * i : 8 * i + 8] for i in range(n)]
    inv = [jnp.where(lane == sub + 8 * i, 1.0, 0.0).astype(F32) for i in range(n)]
    out = []
    for m in range(n):
        if m == n // 2:
            at_half()
        j0 = 8 * m
        top, eye = rows[m], inv[m]
        cols = [jnp.broadcast_to(top[:, j0 + k : j0 + k + 1], full) for k in range(8)]
        e = {(i, k): jnp.broadcast_to(cols[k][i : i + 1], full) for k in range(8) for i in range(k, 8)}
        u = [jnp.broadcast_to(top[i : i + 1], full) for i in range(8)]
        x = [jnp.broadcast_to(eye[i : i + 1], full) for i in range(8)]
        r, low = [None] * 8, {}
        for k in range(8):
            r[k] = lax.rsqrt(e[k, k])
            for i in range(k + 1, 8):
                low[i, k] = e[i, k] * r[k]
            for i in range(k + 1, 8):
                for j in range(k + 1, i + 1):
                    e[i, j] = e[i, j] - low[i, k] * low[j, k]
            u[k] = u[k] * r[k]
            x[k] = x[k] * r[k]
            for i in range(k + 1, 8):
                u[i] = u[i] - low[i, k] * u[k]
                x[i] = x[i] - low[i, k] * x[k]
        done = x[0]
        for k in range(1, 8):
            done = jnp.where(sub == k, x[k], done)
        out.append(done)
        for q in range(m + 1, n):
            src = rows[q]
            t, w, lq = src, inv[q], []
            for k in range(8):
                v = jnp.broadcast_to(src[:, j0 + k : j0 + k + 1], full)
                for p in range(k):
                    v = v - lq[p] * low[k, p]
                v = v * r[k]
                lq.append(v)
                t = t - v * u[k]
                w = w - v * x[k]
            rows[q], inv[q] = t, w
    return jnp.concatenate(out, axis=0)


def factor(a_ref, i_ref, diagonal, others, between):
    n = ORD // BLK

    def step(j, carry):
        jb = pl.multiple_of(j * BLK, BLK)
        diagonal(j)
        for v in range(1, n):

            @pl.when(j == v)
            def _(v=v):
                if v < n - 1:
                    others(v)
                a_ref[BLK * v : BLK * v + BLK, BLK * v :] -= dot_t(
                    a_ref[0 : BLK * v, BLK * v : BLK * v + BLK], a_ref[0 : BLK * v, BLK * v :]
                )

        between(2 * j)
        i_ref[j] = factor_tile(a_ref[pl.ds(jb, BLK), pl.ds(jb, BLK)], lambda: between(2 * j + 1))
        for v in range(n - 1):

            @pl.when(j == v)
            def _(v=v):
                if v == 0:
                    others(v)
                here = (slice(BLK * v, BLK * v + BLK), slice(BLK * v + BLK, ORD))
                a_ref[here] = dot(i_ref[v], a_ref[here])

        return carry

    lax.fori_loop(0, n, step, 0)


def solve(a_ref, i_ref, pairs):
    for j in range(ORD // BLK):
        here = slice(BLK * j, BLK * j + BLK)
        for s_ref, y_ref in pairs:
            acc = s_ref[here, :]
            if j:
                acc = acc - dot_t(a_ref[0 : BLK * j, here], y_ref[0 : BLK * j, :])
            y_ref[here, :] = dot(i_ref[j], acc)


def remote(src, dst, send_sem, recv_sem, dev):
    return pltpu.make_async_remote_copy(
        src_ref=src,
        dst_ref=dst,
        send_sem=send_sem,
        recv_sem=recv_sem,
        device_id=dev,
        device_id_type=MESH,
    )


def each(lo, hi, fn):
    def go(k, carry):
        fn(k)
        return carry

    lax.fori_loop(lo, hi, go, 0)


def rows_of(k):
    return pl.ds(pl.multiple_of(k * PB, PB), PB)


def ring(ref, row, sems):
    rs, rr, ls, lr = sems
    right, left = lax.rem(row + 1, N), lax.rem(row + N - 1, N)

    def to_right(s):
        view = ref.at[rows_of(lax.rem(row - s + N, N)), :]
        return remote(view, view, rs.at[s], rr.at[s], {"row": right})

    def to_left(s):
        view = ref.at[rows_of(lax.rem(row + s, N)), :]
        return remote(view, view, ls.at[s], lr.at[s], {"row": left})

    def got_right(s):
        view = ref.at[rows_of(lax.rem(row - 1 - s + 2 * N, N)), :]
        return remote(view, view, rs.at[s], rr.at[s], {"row": right})

    def got_left(s):
        view = ref.at[rows_of(lax.rem(row + 1 + s, N)), :]
        return remote(view, view, ls.at[s], lr.at[s], {"row": left})

    def start():
        to_right(0).start()
        to_left(0).start()

    def relay(s):
        @pl.when(s < 8)
        def _():
            got_right(s - 1).wait_recv()
            to_right(s).start()

        @pl.when(s < 7)
        def _():
            got_left(s - 1).wait_recv()
            to_left(s).start()

    def finish():
        got_right(7).wait_recv()
        got_left(6).wait_recv()
        each(0, 8, lambda s: to_right(s).wait_send())
        each(0, 7, lambda s: to_left(s).wait_send())

    return start, relay, finish


def packed_piece(tile):
    turned = jnp.transpose(tile)
    lane = lax.broadcasted_iota(jnp.int32, (8, BLK), 1)
    out = turned[0:8]
    for g in range(1, 4):
        out = jnp.where(lane >= PB * g, pltpu.roll(turned[8 * g : 8 * g + 8], PB * g, 1), out)
    return out


def unpack_pieces(pc_ref, rb_ref):
    lane = lax.broadcasted_iota(jnp.int32, (8, BLK), 1)
    for l in range(4):
        pcs = [pc_ref[4 * l + kk] for kk in range(4)]
        for g in range(4):
            out = None
            for kk in range(4):
                shift = (PB * (kk - g)) % BLK
                v = pltpu.roll(pcs[kk], shift, 1) if shift else pcs[kk]
                out = v if kk == 0 else jnp.where(lane >= PB * kk, v, out)
            rb_ref[8 * g : 8 * g + 8, BLK * l : BLK * l + BLK] = out


def greet(devices):
    barrier = pltpu.get_barrier_semaphore()
    total = 0
    for count, dev in devices:
        each(1, count + 1, lambda k, dev=dev: pl.semaphore_signal(barrier, inc=1, device_id=dev(k), device_id_type=MESH))
        total += count
    pl.semaphore_wait(barrier, total)


def row_gather(pc, row, send, recv):
    def to(k):
        return remote(pc.at[row], pc.at[row], send.at[k], recv.at[row], {"row": lax.rem(row + k, N)})

    def got(k):
        view = pc.at[lax.rem(row + k, N)]
        return remote(view, view, send.at[k], recv.at[lax.rem(row + k, N)], {"row": row})

    def start():
        each(1, N, lambda k: to(k).start())

    def wait():
        each(1, N, lambda k: got(k).wait_recv())

    def finish():
        each(1, N, lambda k: to(k).wait_send())

    return start, wait, finish


def corner_gather(rb, a_ref, col, ds, dr, os, orr):
    group = col // 4

    def peer(k):
        return {"col": lax.rem(col + k, N)}

    def tile_lanes(g):
        return pl.ds(pl.multiple_of(g * BLK, BLK), BLK)

    def diag_to(k):
        return remote(
            rb.at[:, tile_lanes(group)], a_ref.at[rows_of(col), tile_lanes(group)], ds.at[k], dr.at[col], peer(k)
        )

    def rest_to(k, v):
        lanes = slice(BLK * v + BLK, ORD)
        return remote(rb.at[:, lanes], a_ref.at[rows_of(col), lanes], os.at[k], orr.at[col], peer(k))

    def start():
        each(1, N, lambda k: diag_to(k).start())
        for v in range(3):

            @pl.when(group == v)
            def _(v=v):
                each(1, N, lambda k: rest_to(k, v).start())

    def diagonal(j):
        def one(i):
            src = 4 * j + i

            @pl.when(src != col)
            def _():
                view = a_ref.at[rows_of(src), tile_lanes(j)]
                remote(view, view, ds.at[0], dr.at[src], {"col": src}).wait_recv()

        each(0, 4, one)

    def others(v):
        def one(i):
            src = 4 * v + i

            @pl.when(src != col)
            def _():
                view = a_ref.at[rows_of(src), BLK * v + BLK : ORD]
                remote(view, view, os.at[0], orr.at[src], {"col": src}).wait_recv()

        each(0, 4, one)

    def finish():
        each(1, N, lambda k: diag_to(k).wait_send())
        for v in range(3):

            @pl.when(group == v)
            def _(v=v):
                each(1, N, lambda k: rest_to(k, v).wait_send())

    return start, diagonal, others, finish


def column_gather(sr, col, send, recv):
    def to(k):
        view = sr.at[rows_of(col), :]
        return remote(view, view, send.at[k], recv.at[col], {"col": lax.rem(col + k, N)})

    def got(k):
        src = lax.rem(col + k, N)
        view = sr.at[rows_of(src), :]
        return remote(view, view, send.at[k], recv.at[src], {"col": col})

    def start():
        each(1, N, lambda k: to(k).start())

    def wait():
        each(1, N, lambda k: got(k).wait_recv())

    def finish():
        each(1, N, lambda k: to(k).wait_send())

    return start, wait, finish


def kernel(
    map_ref, blk_ref, root_ref, panel_ref, rpanel_ref, out_ref,
    pc, rb, a_ref, inv_ref, sc, sr, yr, upd, give, take, rx, cg, ct,
    pc2, rb2, a2, inv2, sc2, sr2, yr2, asm,
    s1, r1, s2, r2, s3, r3, s4, r4, rs, rr, ls, lr, xs, xr,
    s5, r5, s6, r6, s7, r7, s8, r8, rs2, rr2, ls2, lr2,
):
    half, row, col = lax.axis_index("half"), lax.axis_index("row"), lax.axis_index("col")
    other = {"half": 1 - half}
    piece_start, piece_wait, piece_end = row_gather(pc, row, s1, r1)
    block_start, block_diag, block_rest, block_end = corner_gather(rb, a_ref, col, s2, r2, s3, r3)
    column_start, column_wait, column_end = column_gather(sr, col, s4, r4)
    ring_start, relay, ring_end = ring(sc, row, (rs, rr, ls, lr))
    piece_start2, piece_wait2, piece_end2 = row_gather(pc2, row, s5, r5)
    block_start2, block_diag2, block_rest2, block_end2 = corner_gather(rb2, a2, col, s6, r6, s7, r7)
    column_start2, column_wait2, column_end2 = column_gather(sr2, col, s8, r8)
    ring_start2, relay2, ring_end2 = ring(sc2, row, (rs2, rr2, ls2, lr2))

    pc[row] = packed_piece(blk_ref[0:BLK, 0:BLK])
    sc[rows_of(row), :] = blk_ref[0:PB, :]
    greet(
        [
            (N - 1, lambda k: {"row": lax.rem(row + k, N)}),
            (N - 1, lambda k: {"col": lax.rem(col + k, N)}),
            (1, lambda k: other),
        ]
    )
    piece_start()
    ring_start()
    root_corner = remote(root_ref.at[0:PB, 0:BLK], rx, xs.at[0], xr.at[0], other)
    root_corner.start()
    sr[rows_of(col), :] = jnp.concatenate(
        [jnp.transpose(blk_ref[BLK * i : BLK * i + BLK, 0:BLK])[0:PB] for i in range(1, 4)], axis=1
    )
    piece_wait()
    unpack_pieces(pc, rb)
    block_start()
    a_ref[rows_of(col), :] = rb[...]
    relay(1)

    def between(i):
        @pl.when(i == 2)
        def _():
            column_start()

        relay(i + 2)

    factor(a_ref, inv_ref, block_diag, block_rest, between)
    ring_end()
    column_wait()
    solve(a_ref, inv_ref, [(sc, panel_ref), (sr, yr)])

    def source(part, target):
        found = jnp.int32(-1)
        for u in range(3):
            found = jnp.where(map_ref[0, 3 * part + u] == 4 * part + target, jnp.int32(u), found)
        return found

    from_rows = [source(row, a) for a in range(4)]
    theirs = [source(col, 2 * (1 - half) + b) for b in range(2)]
    ours = [source(col, 2 * half + b) for b in range(2)]
    p, q = from_rows[0], source(col, 0)
    inside = jnp.logical_and(p >= 0, q >= 0)

    def pick(which, get):
        return jnp.where(which == 2, get(2), jnp.where(which == 1, get(1), get(0)))

    def lanes(v):
        return slice(BLK + BLK * v, 2 * BLK + BLK * v)

    corner = pick(p, lambda u: pick(q, lambda v: blk_ref[BLK + BLK * u : BLK + BLK * u + PB, lanes(v)])) - dot_t(
        pick(p, lambda u: yr[:, BLK * u : BLK * u + BLK]), pick(q, lambda v: panel_ref[:, lanes(v)])
    )[0:PB]
    cg[...] = jnp.where(inside, corner, 0.0)
    swap_corner = remote(cg, ct, xs.at[1], xr.at[1], other)
    swap_corner.start()
    root_corner.wait_recv()
    base = jnp.where(half == 0, root_ref[0:PB, 0:BLK], rx[...])
    swap_corner.wait_recv()
    corner = base + (cg[...] + ct[...])
    pc2[row] = packed_piece(jnp.concatenate([corner] * 4, axis=0))
    piece_start2()
    for u in range(3):
        rows = slice(BLK * u, BLK * u + BLK)
        block = blk_ref[BLK + BLK * u : 2 * BLK + BLK * u, BLK:] - dot_t(yr[:, rows], panel_ref[:, BLK:])
        for v in range(3):
            upd[3 * u + v] = block[:, BLK * v : BLK * v + BLK]

    def tile(p, q):
        value = upd[jnp.maximum(p, 0) * 3 + jnp.maximum(q, 0)]
        return jnp.where(jnp.logical_and(p >= 0, q >= 0), value, 0.0)

    for a in range(4):
        for b in range(2):
            give[BLK * a : BLK * a + BLK, BLK * b : BLK * b + BLK] = tile(from_rows[a], theirs[b])
    swap = remote(give, take, xs.at[2], xr.at[2], other)
    swap.start()

    piece_wait2()
    unpack_pieces(pc2, rb2)
    block_start2()
    a2[rows_of(col), :] = rb2[...]
    swap.wait_recv()
    for a in range(4):
        for b in range(2):
            at = (slice(BLK * a, BLK * a + BLK), slice(BLK * b, BLK * b + BLK))
            asm[at] = root_ref[at] + (tile(from_rows[a], ours[b]) + take[at])
    sc2[rows_of(row), :] = asm[0:PB, :]
    ring_start2()
    own_columns = sr2.at[rows_of(col), :]
    copy_columns = remote(own_columns, own_columns, xs.at[3], xr.at[3], other)

    @pl.when(half == 0)
    def _():
        sr2[rows_of(col), :] = jnp.concatenate(
            [jnp.transpose(asm[BLK * i : BLK * i + BLK, 0:BLK])[0:PB] for i in range(4)], axis=1
        )
        copy_columns.start()

    def between2(i):
        @pl.when(i == 2)
        def _():
            @pl.when(half == 1)
            def _():
                copy_columns.wait_recv()

            column_start2()

        @pl.when(i > 0)
        def _():
            relay2(i)

    factor(a2, inv2, block_diag2, block_rest2, between2)
    ring_end2()
    column_wait2()
    solve(a2, inv2, [(sc2, rpanel_ref), (sr2, yr2)])
    for i in range(4):
        rows = slice(BLK * i, BLK * i + BLK)
        out_ref[rows, :] = asm[rows, :] - dot_t(yr2[:, rows], rpanel_ref[...])

    @pl.when(half == 0)
    def _():
        copy_columns.wait_send()

    for copy in (root_corner, swap_corner, swap):
        copy.wait_send()
    for end in (piece_end, block_end, column_end, piece_end2, block_end2, column_end2):
        end()


def body(child_front, child_map, root_front):
    sds = jax.ShapeDtypeStruct
    full, side = (ORD, ORD), (ORD, ORD // 2)
    sems = [N] * 8 + [8] * 4 + [4, 4] + [N] * 8 + [8] * 4
    shapes = [
        (N, 8, BLK), (PB, ORD), full, (4, BLK, BLK), full, (ORD, 3 * BLK), (ORD, 3 * BLK), (9, BLK, BLK), side, side,
        (PB, BLK), (PB, BLK), (PB, BLK), (N, 8, BLK), (PB, ORD), full, (4, BLK, BLK), side, full, full, side,
    ]
    panel, root_panel, root_update = pl.pallas_call(
        kernel,
        out_shape=[sds(full, F32), sds(side, F32), sds(side, F32)],
        in_specs=[SM, VM, VM],
        out_specs=[VM, VM, VM],
        scratch_shapes=[*(pltpu.VMEM(s, F32) for s in shapes), *(pltpu.SemaphoreType.DMA((n,)) for n in sems)],
        compiler_params=pltpu.CompilerParams(
            collective_id=0, has_side_effects=True, vmem_limit_bytes=48 * 2**20
        ),
    )(child_map, child_front[0], root_front.reshape(side))
    return (panel[None], root_panel[:, None, None, :], root_update[:, None, None, :])


def solution(mesh):
    return jax.shard_map(
        body,
        mesh=mesh,
        in_specs=(P("half", "row", "col"), P("half", None), P("row", "col", "half", None)),
        out_specs=(
            P("half", None, "col"),
            P(None, "col", "half", None),
            P("row", "col", "half", None),
        ),
        check_vma=False,
    )
```

```python
import jax
import jax.numpy as jnp
from jax import lax
from jax.experimental import pallas as pl
from jax.experimental.pallas import tpu as pltpu
from jax.sharding import PartitionSpec as P

N = 16
PB = 32
BLK = 128
ORD = N * PB
F32 = jnp.float32
MESH = pl.DeviceIdType.MESH
VM = pl.BlockSpec(memory_space=pltpu.VMEM)
SM = pl.BlockSpec(memory_space=pltpu.SMEM)


def dot(a, b):
    return lax.dot_general(
        a, b, (((1,), (0,)), ((), ())), precision=lax.Precision.HIGHEST, preferred_element_type=F32
    )


def dot_t(a, b):
    return lax.dot_general(
        a, b, (((0,), (0,)), ((), ())), precision=lax.Precision.HIGHEST, preferred_element_type=F32
    )


def factor_tile(a, at_half):
    n, full = BLK // 8, (8, BLK)
    diag = lax.broadcasted_iota(jnp.int32, (BLK, BLK), 0) == lax.broadcasted_iota(jnp.int32, (BLK, BLK), 1)
    only = jnp.where(diag, a, 0.0)
    scale = lax.rsqrt(jnp.sum(only, axis=0, keepdims=True))
    a = a * lax.rsqrt(jnp.sum(only, axis=1, keepdims=True)) * scale
    lane = lax.broadcasted_iota(jnp.int32, full, 1)
    sub = lax.broadcasted_iota(jnp.int32, full, 0)
    rows = [a[8 * i : 8 * i + 8] for i in range(n)]
    out = []
    for m in range(n):
        if m == n // 2:
            at_half()
        j0 = 8 * m
        left = lane < j0 + 8
        pivots = jnp.logical_and(lane >= j0, left)
        cols = [jnp.broadcast_to(rows[m][:, j0 + k : j0 + k + 1], full) for k in range(8)]
        e = {(i, k): jnp.broadcast_to(cols[k][i : i + 1], full) for k in range(8) for i in range(k, 8)}
        top = jnp.where(pivots, jnp.where(lane == sub + j0, 1.0, 0.0), rows[m])
        u = [jnp.broadcast_to(top[i : i + 1], full) for i in range(8)]
        r, low = [None] * 8, {}
        for k in range(0, 8, 2):
            pa, pb, pc = e[k, k], e[k + 1, k], e[k + 1, k + 1]
            r[k] = lax.rsqrt(pa)
            r[k + 1] = lax.rsqrt(pa * pc - pb * pb) * (pa * r[k])
            for i in range(k + 1, 8):
                low[i, k] = e[i, k] * r[k]
            for i in range(k + 2, 8):
                low[i, k + 1] = (e[i, k + 1] - low[i, k] * low[k + 1, k]) * r[k + 1]
            for i in range(k + 2, 8):
                for j in range(k + 2, i + 1):
                    e[i, j] = (e[i, j] - low[i, k] * low[j, k]) - low[i, k + 1] * low[j, k + 1]
            for p in (k, k + 1):
                u[p] = u[p] * r[p]
                for i in range(p + 1, 8):
                    u[i] = u[i] - low[i, p] * u[p]
        done = u[0]
        for k in range(1, 8):
            done = jnp.where(sub == k, u[k], done)
        out.append(jnp.where(left, done, 0.0))
        for q in range(m + 1, n):
            src = rows[q]
            t, lq = jnp.where(pivots, 0.0, src), []
            for k in range(8):
                v = jnp.broadcast_to(src[:, j0 + k : j0 + k + 1], full)
                for p in range(k):
                    v = v - lq[p] * low[k, p]
                v = v * r[k]
                lq.append(v)
                t = t - v * u[k]
            rows[q] = t
    return jnp.concatenate(out, axis=0) * scale


def factor(a_ref, i_ref, diagonal, others, between):
    n = ORD // BLK

    def step(j, carry):
        jb = pl.multiple_of(j * BLK, BLK)
        diagonal(j)
        for v in range(1, n):

            @pl.when(j == v)
            def _(v=v):
                if v < n - 1:
                    others(v)
                a_ref[BLK * v : BLK * v + BLK, BLK * v :] -= dot_t(
                    a_ref[0 : BLK * v, BLK * v : BLK * v + BLK], a_ref[0 : BLK * v, BLK * v :]
                )

        between(2 * j)
        i_ref[j] = factor_tile(a_ref[pl.ds(jb, BLK), pl.ds(jb, BLK)], lambda: between(2 * j + 1))
        for v in range(n - 1):

            @pl.when(j == v)
            def _(v=v):
                if v == 0:
                    others(v)
                here = (slice(BLK * v, BLK * v + BLK), slice(BLK * v + BLK, ORD))
                a_ref[here] = dot(i_ref[v], a_ref[here])

        return carry

    lax.fori_loop(0, n, step, 0)


def solve(a_ref, i_ref, pairs):
    for j in range(ORD // BLK):
        here = slice(BLK * j, BLK * j + BLK)
        for s_ref, y_ref in pairs:
            acc = s_ref[here, :]
            if j:
                acc = acc - dot_t(a_ref[0 : BLK * j, here], y_ref[0 : BLK * j, :])
            y_ref[here, :] = dot(i_ref[j], acc)


def remote(src, dst, send_sem, recv_sem, dev):
    return pltpu.make_async_remote_copy(
        src_ref=src,
        dst_ref=dst,
        send_sem=send_sem,
        recv_sem=recv_sem,
        device_id=dev,
        device_id_type=MESH,
    )


def each(lo, hi, fn):
    def go(k, carry):
        fn(k)
        return carry

    lax.fori_loop(lo, hi, go, 0)


def rows_of(k):
    return pl.ds(pl.multiple_of(k * PB, PB), PB)


def ring(ref, row, sems):
    rs, rr, ls, lr = sems
    right, left = {"row": lax.rem(row + 1, N)}, {"row": lax.rem(row + N - 1, N)}
    wide = ref.shape[1] // 2

    def part(block, p):
        return ref.at[rows_of(block), wide * p : wide * p + wide]

    def to_right(s, p):
        view = part(lax.rem(row - s + N, N), p)
        return remote(view, view, rs.at[2 * s + p], rr.at[2 * s + p], right)

    def to_left(s, p):
        view = part(lax.rem(row + s, N), p)
        return remote(view, view, ls.at[2 * s + p], lr.at[2 * s + p], left)

    def got_right(s, p):
        view = part(lax.rem(row - 1 - s + 2 * N, N), p)
        return remote(view, view, rs.at[2 * s + p], rr.at[2 * s + p], right)

    def got_left(s, p):
        view = part(lax.rem(row + 1 + s, N), p)
        return remote(view, view, ls.at[2 * s + p], lr.at[2 * s + p], left)

    def start():
        for p in range(2):
            to_right(0, p).start()
            to_left(0, p).start()

    def relay(s):
        @pl.when(s < 7)
        def _():
            for p in range(2):
                got_right(s - 1, p).wait_recv()
                to_right(s, p).start()
                got_left(s - 1, p).wait_recv()
                to_left(s, p).start()

        @pl.when(s == 7)
        def _():
            for p in range(2):
                got_right(s - 1, p).wait_recv()
                to_right(s, p).start()

    def finish():
        for p in range(2):
            got_right(7, p).wait_recv()
            got_left(6, p).wait_recv()
        for p in range(2):
            each(0, 8, lambda s, p=p: to_right(s, p).wait_send())
            each(0, 7, lambda s, p=p: to_left(s, p).wait_send())

    return start, relay, finish


def packed_piece(tile):
    turned = jnp.transpose(tile)
    lane = lax.broadcasted_iota(jnp.int32, (8, BLK), 1)
    out = turned[0:8]
    for g in range(1, 4):
        out = jnp.where(lane >= PB * g, pltpu.roll(turned[8 * g : 8 * g + 8], PB * g, 1), out)
    return out


def unpack_pieces(pc_ref, rb_ref):
    lane = lax.broadcasted_iota(jnp.int32, (8, BLK), 1)
    for l in range(4):
        pcs = [pc_ref[4 * l + kk] for kk in range(4)]
        for g in range(4):
            out = None
            for kk in range(4):
                shift = (PB * (kk - g)) % BLK
                v = pltpu.roll(pcs[kk], shift, 1) if shift else pcs[kk]
                out = v if kk == 0 else jnp.where(lane >= PB * kk, v, out)
            rb_ref[8 * g : 8 * g + 8, BLK * l : BLK * l + BLK] = out


def greet(devices):
    barrier = pltpu.get_barrier_semaphore()
    for count, dev in devices:
        each(1, count + 1, lambda k, dev=dev: pl.semaphore_signal(barrier, inc=1, device_id=dev(k), device_id_type=MESH))
    return lambda: pl.semaphore_wait(barrier, sum(count for count, _ in devices))


def row_gather(pc, row, send, recv):
    def to(k):
        return remote(pc.at[row], pc.at[row], send.at[k], recv.at[row], {"row": lax.rem(row + k, N)})

    def got(k):
        view = pc.at[lax.rem(row + k, N)]
        return remote(view, view, send.at[k], recv.at[lax.rem(row + k, N)], {"row": row})

    def start():
        each(1, N, lambda k: to(k).start())

    def wait():
        each(1, N, lambda k: got(k).wait_recv())

    def finish():
        each(1, N, lambda k: to(k).wait_send())

    return start, wait, finish


def corner_gather(rb, a_ref, col, ds, dr, os, orr):
    group = col // 4

    def peer(k):
        return {"col": lax.rem(col + k, N)}

    def tile_lanes(g):
        return pl.ds(pl.multiple_of(g * BLK, BLK), BLK)

    def diag_to(k):
        return remote(
            rb.at[:, tile_lanes(group)], a_ref.at[rows_of(col), tile_lanes(group)], ds.at[k], dr.at[col], peer(k)
        )

    def rest_to(k, v):
        lanes = slice(BLK * v + BLK, ORD)
        return remote(rb.at[:, lanes], a_ref.at[rows_of(col), lanes], os.at[k], orr.at[col], peer(k))

    def start(v):
        @pl.when(group == v)
        def _():
            each(1, N, lambda k: diag_to(k).start())
            if v < 3:
                each(1, N, lambda k: rest_to(k, v).start())

    def diagonal(j):
        def one(i):
            src = 4 * j + i

            @pl.when(src != col)
            def _():
                view = a_ref.at[rows_of(src), tile_lanes(j)]
                remote(view, view, ds.at[0], dr.at[src], {"col": src}).wait_recv()

        each(0, 4, one)

    def others(v):
        def one(i):
            src = 4 * v + i

            @pl.when(src != col)
            def _():
                view = a_ref.at[rows_of(src), BLK * v + BLK : ORD]
                remote(view, view, os.at[0], orr.at[src], {"col": src}).wait_recv()

        each(0, 4, one)

    def finish():
        each(1, N, lambda k: diag_to(k).wait_send())
        for v in range(3):

            @pl.when(group == v)
            def _(v=v):
                each(1, N, lambda k: rest_to(k, v).wait_send())

    return start, diagonal, others, finish


def column_gather(sr, col, send, recv):
    def to(k):
        view = sr.at[rows_of(col), :]
        return remote(view, view, send.at[k], recv.at[col], {"col": lax.rem(col + k, N)})

    def got(k):
        src = lax.rem(col + k, N)
        view = sr.at[rows_of(src), :]
        return remote(view, view, send.at[k], recv.at[src], {"col": col})

    def start():
        each(1, N, lambda k: to(k).start())

    def wait():
        each(1, N, lambda k: got(k).wait_recv())

    def finish():
        each(1, N, lambda k: to(k).wait_send())

    return start, wait, finish


def split_sides(src, dst):
    for t in range(2):
        dst[:, BLK * t : BLK * t + BLK] = src[pl.ds(t, ORD, stride=2), :]


def kernel(
    map_ref, blk_ref, root_ref, panel_ref, rpanel_ref, out_ref,
    pc, rb, a_ref, inv_ref, sc, sr, yr, upd, give, take, rx, cg, ct,
    pc2, rb2, a2, inv2, sc2, sr2, yr2, asm, root, rp,
    s1, r1, s2, r2, s3, r3, s4, r4, rs, rr, ls, lr, xs, xr,
    s5, r5, s6, r6, s7, r7, s8, r8, rs2, rr2, ls2, lr2,
):
    half, row, col = lax.axis_index("half"), lax.axis_index("row"), lax.axis_index("col")
    other = {"half": 1 - half}
    piece_start, piece_wait, piece_end = row_gather(pc, row, s1, r1)
    block_start, block_diag, block_rest, block_end = corner_gather(rb, a_ref, col, s2, r2, s3, r3)
    column_start, column_wait, column_end = column_gather(sr, col, s4, r4)
    ring_start, relay, ring_end = ring(sc, row, (rs, rr, ls, lr))
    piece_start2, piece_wait2, piece_end2 = row_gather(pc2, row, s5, r5)
    block_start2, block_diag2, block_rest2, block_end2 = corner_gather(rb2, a2, col, s6, r6, s7, r7)
    column_start2, column_wait2, column_end2 = column_gather(sr2, col, s8, r8)
    ring_start2, relay2, ring_end2 = ring(sc2, row, (rs2, rr2, ls2, lr2))

    wait_all = greet(
        [
            (N - 1, lambda k: {"row": lax.rem(row + k, N)}),
            (N - 1, lambda k: {"col": lax.rem(col + k, N)}),
            (1, lambda k: other),
        ]
    )
    pc[row] = packed_piece(blk_ref[0:BLK, 0:BLK])
    sc[rows_of(row), :] = blk_ref[0:PB, :]
    sr[rows_of(col), :] = jnp.concatenate(
        [jnp.transpose(blk_ref[BLK * i : BLK * i + BLK, 0:BLK])[0:PB] for i in range(1, 4)], axis=1
    )
    split_sides(root_ref, root)
    wait_all()
    piece_start()
    ring_start()
    root_corner = remote(root.at[0:PB, 0:BLK], rx, xs.at[0], xr.at[0], other)
    root_corner.start()
    piece_wait()
    unpack_pieces(pc, rb)
    block_start(0)
    block_start(1)
    a_ref[rows_of(col), :] = rb[...]
    relay(1)

    def between(i):
        for v in (2, 3):

            @pl.when(i == v - 2)
            def _(v=v):
                block_start(v)

        @pl.when(i == 2)
        def _():
            column_start()

        relay(i + 2)

    factor(a_ref, inv_ref, block_diag, block_rest, between)
    ring_end()
    column_wait()
    solve(a_ref, inv_ref, [(sc, panel_ref), (sr, yr)])

    def source(part, target):
        found = jnp.int32(-1)
        for u in range(3):
            found = jnp.where(map_ref[0, 3 * part + u] == 4 * part + target, jnp.int32(u), found)
        return found

    from_rows = [source(row, a) for a in range(4)]
    theirs = [source(col, 2 * (1 - half) + b) for b in range(2)]
    ours = [source(col, 2 * half + b) for b in range(2)]
    p, q = from_rows[0], source(col, 0)
    inside = jnp.logical_and(p >= 0, q >= 0)

    def pick(which, get):
        return jnp.where(which == 2, get(2), jnp.where(which == 1, get(1), get(0)))

    def lanes(v):
        return slice(BLK + BLK * v, 2 * BLK + BLK * v)

    corner = pick(p, lambda u: pick(q, lambda v: blk_ref[BLK + BLK * u : BLK + BLK * u + PB, lanes(v)])) - dot_t(
        pick(p, lambda u: yr[:, BLK * u : BLK * u + BLK]), pick(q, lambda v: panel_ref[:, lanes(v)])
    )[0:PB]
    cg[...] = jnp.where(inside, corner, 0.0)
    swap_corner = remote(cg, ct, xs.at[1], xr.at[1], other)
    swap_corner.start()
    root_corner.wait_recv()
    base = jnp.where(half == 0, root[0:PB, 0:BLK], rx[...])
    swap_corner.wait_recv()
    corner = base + (cg[...] + ct[...])
    pc2[row] = packed_piece(jnp.concatenate([corner] * 4, axis=0))
    piece_start2()
    for u in range(3):
        rows = slice(BLK * u, BLK * u + BLK)
        block = blk_ref[BLK + BLK * u : 2 * BLK + BLK * u, BLK:] - dot_t(yr[:, rows], panel_ref[:, BLK:])
        for v in range(3):
            upd[3 * u + v] = block[:, BLK * v : BLK * v + BLK]

    def tile(p, q):
        value = upd[jnp.maximum(p, 0) * 3 + jnp.maximum(q, 0)]
        return jnp.where(jnp.logical_and(p >= 0, q >= 0), value, 0.0)

    for a in range(4):
        for b in range(2):
            give[BLK * a : BLK * a + BLK, BLK * b : BLK * b + BLK] = tile(from_rows[a], theirs[b])
    swap = remote(give, take, xs.at[2], xr.at[2], other)
    swap.start()

    piece_wait2()
    unpack_pieces(pc2, rb2)
    block_start2(0)
    block_start2(1)
    a2[rows_of(col), :] = rb2[...]
    swap.wait_recv()
    for a in range(4):
        for b in range(2):
            at = (slice(BLK * a, BLK * a + BLK), slice(BLK * b, BLK * b + BLK))
            asm[at] = root[at] + (tile(from_rows[a], ours[b]) + take[at])
    sc2[rows_of(row), :] = asm[0:PB, :]
    ring_start2()
    own_columns = sr2.at[rows_of(col), :]
    copy_columns = remote(own_columns, own_columns, xs.at[3], xr.at[3], other)

    @pl.when(half == 0)
    def _():
        sr2[rows_of(col), :] = jnp.concatenate(
            [jnp.transpose(asm[BLK * i : BLK * i + BLK, 0:BLK])[0:PB] for i in range(4)], axis=1
        )
        copy_columns.start()

    def between2(i):
        for v in (2, 3):

            @pl.when(i == v - 2)
            def _(v=v):
                block_start2(v)

        @pl.when(i == 2)
        def _():
            @pl.when(half == 1)
            def _():
                copy_columns.wait_recv()

            column_start2()

        @pl.when(i > 0)
        def _():
            relay2(i)

    factor(a2, inv2, block_diag2, block_rest2, between2)
    ring_end2()
    column_wait2()
    solve(a2, inv2, [(sc2, rp), (sr2, yr2)])
    for t in range(2):
        rpanel_ref[pl.ds(t, ORD, stride=2), :] = rp[:, BLK * t : BLK * t + BLK]
    for i in range(4):
        rows = slice(BLK * i, BLK * i + BLK)
        block = asm[rows, :] - dot_t(yr2[:, rows], rp[...])
        for t in range(2):
            out_ref[pl.ds(2 * BLK * i + t, BLK, stride=2), :] = block[:, BLK * t : BLK * t + BLK]

    @pl.when(half == 0)
    def _():
        copy_columns.wait_send()

    for copy in (root_corner, swap_corner, swap):
        copy.wait_send()
    for end in (piece_end, block_end, column_end, piece_end2, block_end2, column_end2):
        end()


def body(child_front, child_map, root_front):
    sds = jax.ShapeDtypeStruct
    full, side = (ORD, ORD), (ORD, ORD // 2)
    sems = [N] * 12 + [4, 4] + [N] * 12
    shapes = [
        (N, 8, BLK), (PB, ORD), full, (4, BLK, BLK), full, (ORD, 3 * BLK), (ORD, 3 * BLK), (9, BLK, BLK), side, side,
        (PB, BLK), (PB, BLK), (PB, BLK), (N, 8, BLK), (PB, ORD), full, (4, BLK, BLK), side, full, full, side, side, side,
    ]
    panel, root_panel, root_update = pl.pallas_call(
        kernel,
        out_shape=[sds(full, F32), sds((2 * ORD, BLK), F32), sds((2 * ORD, BLK), F32)],
        in_specs=[SM, VM, VM],
        out_specs=[VM, VM, VM],
        scratch_shapes=[*(pltpu.VMEM(s, F32) for s in shapes), *(pltpu.SemaphoreType.DMA((n,)) for n in sems)],
        compiler_params=pltpu.CompilerParams(
            collective_id=0, has_side_effects=True, vmem_limit_bytes=48 * 2**20
        ),
    )(child_map, child_front[0], root_front.reshape(2 * ORD, BLK))
    out = (ORD, 1, 1, ORD // 2)
    return (panel[None], root_panel.reshape(out), root_update.reshape(out))


def solution(mesh):
    return jax.shard_map(
        body,
        mesh=mesh,
        in_specs=(P("half", "row", "col"), P("half", None), P("row", "col", "half", None)),
        out_specs=(
            P("half", None, "col"),
            P(None, "col", "half", None),
            P("row", "col", "half", None),
        ),
        check_vma=False,
    )
```

```python
import jax
import jax.numpy as jnp
from jax import lax
from jax.experimental import pallas as pl
from jax.experimental.pallas import tpu as pltpu
from jax.sharding import PartitionSpec as P

N = 16
PB = 32
BLK = 128
ORD = N * PB
F32 = jnp.float32
MESH = pl.DeviceIdType.MESH
VM = pl.BlockSpec(memory_space=pltpu.VMEM)
SM = pl.BlockSpec(memory_space=pltpu.SMEM)


def dot(a, b):
    return lax.dot_general(
        a, b, (((1,), (0,)), ((), ())), precision=lax.Precision.HIGHEST, preferred_element_type=F32
    )


def dot_t(a, b):
    return lax.dot_general(
        a, b, (((0,), (0,)), ((), ())), precision=lax.Precision.HIGHEST, preferred_element_type=F32
    )


def factor_tile(a, at_half):
    n, full = BLK // 8, (8, BLK)
    diag = lax.broadcasted_iota(jnp.int32, (BLK, BLK), 0) == lax.broadcasted_iota(jnp.int32, (BLK, BLK), 1)
    only = jnp.where(diag, a, 0.0)
    scale = lax.rsqrt(jnp.sum(only, axis=0, keepdims=True))
    a = a * lax.rsqrt(jnp.sum(only, axis=1, keepdims=True)) * scale
    lane = lax.broadcasted_iota(jnp.int32, full, 1)
    sub = lax.broadcasted_iota(jnp.int32, full, 0)
    rows = [a[8 * i : 8 * i + 8] for i in range(n)]
    out = []
    for m in range(n):
        if m == n // 2:
            at_half()
        j0 = 8 * m
        left = lane < j0 + 8
        pivots = jnp.logical_and(lane >= j0, left)
        cols = [jnp.broadcast_to(rows[m][:, j0 + k : j0 + k + 1], full) for k in range(8)]
        e = {(i, k): jnp.broadcast_to(cols[k][i : i + 1], full) for k in range(8) for i in range(k, 8)}
        top = jnp.where(pivots, jnp.where(lane == sub + j0, 1.0, 0.0), rows[m])
        u = [jnp.broadcast_to(top[i : i + 1], full) for i in range(8)]
        r, low = [None] * 8, {}
        for k in range(0, 8, 2):
            pa, pb, pc = e[k, k], e[k + 1, k], e[k + 1, k + 1]
            r[k] = lax.rsqrt(pa)
            r[k + 1] = lax.rsqrt(pa * pc - pb * pb) * (pa * r[k])
            for i in range(k + 1, 8):
                low[i, k] = e[i, k] * r[k]
            for i in range(k + 2, 8):
                low[i, k + 1] = (e[i, k + 1] - low[i, k] * low[k + 1, k]) * r[k + 1]
            for i in range(k + 2, 8):
                for j in range(k + 2, i + 1):
                    e[i, j] = (e[i, j] - low[i, k] * low[j, k]) - low[i, k + 1] * low[j, k + 1]
            for p in (k, k + 1):
                u[p] = u[p] * r[p]
                for i in range(p + 1, 8):
                    u[i] = u[i] - low[i, p] * u[p]
        done = u[0]
        for k in range(1, 8):
            done = jnp.where(sub == k, u[k], done)
        out.append(jnp.where(left, done, 0.0))
        for q in range(m + 1, n):
            src = rows[q]
            t, lq = jnp.where(pivots, 0.0, src), []
            for k in range(8):
                v = jnp.broadcast_to(src[:, j0 + k : j0 + k + 1], full)
                for p in range(k):
                    v = v - lq[p] * low[k, p]
                v = v * r[k]
                lq.append(v)
                t = t - v * u[k]
            rows[q] = t
    return jnp.concatenate(out, axis=0) * scale


def factor(a_ref, i_ref, arrived, between):
    n = ORD // BLK

    def tiles(v):
        return slice(BLK * v, BLK * v + BLK)

    def turn(v):
        for i in range(v + 1, n):
            arrived(v, i)
        for i in range(v + 1, n):
            a_ref[tiles(v), tiles(i)] = jnp.transpose(a_ref[tiles(i), tiles(v)])

    def step(j, carry):
        jb = pl.multiple_of(j * BLK, BLK)
        arrived(j, j)
        for v in range(1, n):

            @pl.when(j == v)
            def _(v=v):
                turn(v)
                a_ref[tiles(v), BLK * v :] -= dot_t(a_ref[0 : BLK * v, tiles(v)], a_ref[0 : BLK * v, BLK * v :])

        between(2 * j)
        i_ref[j] = factor_tile(a_ref[pl.ds(jb, BLK), pl.ds(jb, BLK)], lambda: between(2 * j + 1))
        for v in range(n - 1):

            @pl.when(j == v)
            def _(v=v):
                if v == 0:
                    turn(v)
                here = (tiles(v), slice(BLK * v + BLK, ORD))
                a_ref[here] = dot(i_ref[v], a_ref[here])

        return carry

    lax.fori_loop(0, n, step, 0)


def solve(a_ref, i_ref, pairs):
    for j in range(ORD // BLK):
        here = slice(BLK * j, BLK * j + BLK)
        for s_ref, y_ref in pairs:
            acc = s_ref[here, :]
            if j:
                acc = acc - dot_t(a_ref[0 : BLK * j, here], y_ref[0 : BLK * j, :])
            y_ref[here, :] = dot(i_ref[j], acc)


def remote(src, dst, send_sem, recv_sem, dev):
    return pltpu.make_async_remote_copy(
        src_ref=src,
        dst_ref=dst,
        send_sem=send_sem,
        recv_sem=recv_sem,
        device_id=dev,
        device_id_type=MESH,
    )


def each(lo, hi, fn):
    def go(k, carry):
        fn(k)
        return carry

    lax.fori_loop(lo, hi, go, 0)


def rows_of(k):
    return pl.ds(pl.multiple_of(k * PB, PB), PB)


def ring(ref, row, sems):
    rs, rr, ls, lr = sems
    right, left = {"row": lax.rem(row + 1, N)}, {"row": lax.rem(row + N - 1, N)}
    wide = ref.shape[1] // 2

    def part(block, p):
        return ref.at[rows_of(block), wide * p : wide * p + wide]

    def to_right(s, p):
        view = part(lax.rem(row - s + N, N), p)
        return remote(view, view, rs.at[2 * s + p], rr.at[2 * s + p], right)

    def to_left(s, p):
        view = part(lax.rem(row + s, N), p)
        return remote(view, view, ls.at[2 * s + p], lr.at[2 * s + p], left)

    def got_right(s, p):
        view = part(lax.rem(row - 1 - s + 2 * N, N), p)
        return remote(view, view, rs.at[2 * s + p], rr.at[2 * s + p], right)

    def got_left(s, p):
        view = part(lax.rem(row + 1 + s, N), p)
        return remote(view, view, ls.at[2 * s + p], lr.at[2 * s + p], left)

    def start():
        for p in range(2):
            to_right(0, p).start()
            to_left(0, p).start()

    def relay(s):
        @pl.when(s < 7)
        def _():
            for p in range(2):
                got_right(s - 1, p).wait_recv()
                to_right(s, p).start()
                got_left(s - 1, p).wait_recv()
                to_left(s, p).start()

        @pl.when(s == 7)
        def _():
            for p in range(2):
                got_right(s - 1, p).wait_recv()
                to_right(s, p).start()

    def finish():
        for p in range(2):
            got_right(7, p).wait_recv()
            got_left(6, p).wait_recv()
        for p in range(2):
            each(0, 8, lambda s, p=p: to_right(s, p).wait_send())
            each(0, 7, lambda s, p=p: to_left(s, p).wait_send())

    return start, relay, finish


def packed_piece(tile):
    turned = jnp.transpose(tile)
    lane = lax.broadcasted_iota(jnp.int32, (8, BLK), 1)
    out = turned[0:8]
    for g in range(1, 4):
        out = jnp.where(lane >= PB * g, pltpu.roll(turned[8 * g : 8 * g + 8], PB * g, 1), out)
    return out


def unpack_pieces(pc_ref, rb_ref):
    lane = lax.broadcasted_iota(jnp.int32, (8, BLK), 1)
    for l in range(4):
        pcs = [pc_ref[4 * l + kk] for kk in range(4)]
        for g in range(4):
            out = None
            for kk in range(4):
                shift = (PB * (kk - g)) % BLK
                v = pltpu.roll(pcs[kk], shift, 1) if shift else pcs[kk]
                out = v if kk == 0 else jnp.where(lane >= PB * kk, v, out)
            rb_ref[8 * g : 8 * g + 8, BLK * l : BLK * l + BLK] = out


def greet(devices):
    barrier = pltpu.get_barrier_semaphore()
    for count, dev in devices:
        each(1, count + 1, lambda k, dev=dev: pl.semaphore_signal(barrier, inc=1, device_id=dev(k), device_id_type=MESH))
    return lambda: pl.semaphore_wait(barrier, sum(count for count, _ in devices))


def row_gather(pc, row, send, recv):
    def to(k):
        return remote(pc.at[row], pc.at[row], send.at[k], recv.at[row], {"row": lax.rem(row + k, N)})

    def got(k):
        view = pc.at[lax.rem(row + k, N)]
        return remote(view, view, send.at[k], recv.at[lax.rem(row + k, N)], {"row": row})

    def start():
        each(1, N, lambda k: to(k).start())

    def wait():
        each(1, N, lambda k: got(k).wait_recv())

    def finish():
        each(1, N, lambda k: to(k).wait_send())

    return start, wait, finish


def corner_gather(rb, a_ref, col, send, recv):
    group = col // 4

    def lanes(v):
        return pl.ds(pl.multiple_of(v * BLK, BLK), BLK)

    def to(k, v):
        dst = a_ref.at[rows_of(col), lanes(v)]
        return remote(
            rb.at[:, lanes(v)], dst, send.at[v * N + k], recv.at[v * N + col], {"col": lax.rem(col + k, N)}
        )

    def start(v):
        @pl.when(group >= v)
        def _():
            each(1, N, lambda k: to(k, v).start())

    def arrived(v, g):
        def one(i):
            src = 4 * g + i

            @pl.when(src != col)
            def _():
                view = a_ref.at[rows_of(src), lanes(v)]
                remote(view, view, send.at[0], recv.at[v * N + src], {"col": src}).wait_recv()

        each(0, 4, one)

    def finish():
        for v in range(4):

            @pl.when(group >= v)
            def _(v=v):
                each(1, N, lambda k: to(k, v).wait_send())

    return start, arrived, finish


def column_gather(sr, col, send, recv):
    def to(k):
        view = sr.at[rows_of(col), :]
        return remote(view, view, send.at[k], recv.at[col], {"col": lax.rem(col + k, N)})

    def got(k):
        src = lax.rem(col + k, N)
        view = sr.at[rows_of(src), :]
        return remote(view, view, send.at[k], recv.at[src], {"col": col})

    def start():
        each(1, N, lambda k: to(k).start())

    def wait():
        each(1, N, lambda k: got(k).wait_recv())

    def finish():
        each(1, N, lambda k: to(k).wait_send())

    return start, wait, finish


def split_sides(src, dst):
    for t in range(2):
        dst[:, BLK * t : BLK * t + BLK] = src[pl.ds(t, ORD, stride=2), :]


def kernel(
    map_ref, blk_ref, root_ref, panel_ref, rpanel_ref, out_ref,
    pc, rb, a_ref, inv_ref, sc, sr, yr, upd, give, take, rx, cg, ct,
    pc2, rb2, a2, inv2, sc2, sr2, yr2, asm, root, rp,
    s1, r1, s2, r2, s4, r4, rs, rr, ls, lr, xs, xr,
    s5, r5, s6, r6, s8, r8, rs2, rr2, ls2, lr2,
):
    half, row, col = lax.axis_index("half"), lax.axis_index("row"), lax.axis_index("col")
    other = {"half": 1 - half}
    piece_start, piece_wait, piece_end = row_gather(pc, row, s1, r1)
    block_start, block_arrived, block_end = corner_gather(rb, a_ref, col, s2, r2)
    column_start, column_wait, column_end = column_gather(sr, col, s4, r4)
    ring_start, relay, ring_end = ring(sc, row, (rs, rr, ls, lr))
    piece_start2, piece_wait2, piece_end2 = row_gather(pc2, row, s5, r5)
    block_start2, block_arrived2, block_end2 = corner_gather(rb2, a2, col, s6, r6)
    column_start2, column_wait2, column_end2 = column_gather(sr2, col, s8, r8)
    ring_start2, relay2, ring_end2 = ring(sc2, row, (rs2, rr2, ls2, lr2))

    wait_all = greet(
        [
            (N - 1, lambda k: {"row": lax.rem(row + k, N)}),
            (N - 1, lambda k: {"col": lax.rem(col + k, N)}),
            (1, lambda k: other),
        ]
    )
    pc[row] = packed_piece(blk_ref[0:BLK, 0:BLK])
    sc[rows_of(row), :] = blk_ref[0:PB, :]
    sr[rows_of(col), :] = jnp.concatenate(
        [jnp.transpose(blk_ref[BLK * i : BLK * i + BLK, 0:BLK])[0:PB] for i in range(1, 4)], axis=1
    )
    split_sides(root_ref, root)
    wait_all()
    piece_start()
    ring_start()
    root_corner = remote(root.at[0:PB, 0:BLK], rx, xs.at[0], xr.at[0], other)
    root_corner.start()
    relay(1)
    piece_wait()
    unpack_pieces(pc, rb)
    block_start(0)
    a_ref[rows_of(col), :] = rb[...]
    relay(2)
    relay(3)

    def between(i):
        for v in (1, 2, 3):

            @pl.when(i == v - 1)
            def _(v=v):
                block_start(v)

        @pl.when(i == 3)
        def _():
            column_start()

        relay(i + 4)

    factor(a_ref, inv_ref, block_arrived, between)
    ring_end()
    column_wait()
    solve(a_ref, inv_ref, [(sc, panel_ref), (sr, yr)])

    def source(part, target):
        found = jnp.int32(-1)
        for u in range(3):
            found = jnp.where(map_ref[0, 3 * part + u] == 4 * part + target, jnp.int32(u), found)
        return found

    from_rows = [source(row, a) for a in range(4)]
    theirs = [source(col, 2 * (1 - half) + b) for b in range(2)]
    ours = [source(col, 2 * half + b) for b in range(2)]
    p, q = from_rows[0], source(col, 0)
    inside = jnp.logical_and(p >= 0, q >= 0)

    def pick(which, get):
        return jnp.where(which == 2, get(2), jnp.where(which == 1, get(1), get(0)))

    def lanes(v):
        return slice(BLK + BLK * v, 2 * BLK + BLK * v)

    corner = pick(p, lambda u: pick(q, lambda v: blk_ref[BLK + BLK * u : BLK + BLK * u + PB, lanes(v)])) - dot_t(
        pick(p, lambda u: yr[:, BLK * u : BLK * u + BLK]), pick(q, lambda v: panel_ref[:, lanes(v)])
    )[0:PB]
    cg[...] = jnp.where(inside, corner, 0.0)
    swap_corner = remote(cg, ct, xs.at[1], xr.at[1], other)
    swap_corner.start()
    root_corner.wait_recv()
    base = jnp.where(half == 0, root[0:PB, 0:BLK], rx[...])
    swap_corner.wait_recv()
    corner = base + (cg[...] + ct[...])
    pc2[row] = packed_piece(jnp.concatenate([corner] * 4, axis=0))
    piece_start2()
    for u in range(3):
        rows = slice(BLK * u, BLK * u + BLK)
        block = blk_ref[BLK + BLK * u : 2 * BLK + BLK * u, BLK:] - dot_t(yr[:, rows], panel_ref[:, BLK:])
        for v in range(3):
            upd[3 * u + v] = block[:, BLK * v : BLK * v + BLK]

    def tile(p, q):
        value = upd[jnp.maximum(p, 0) * 3 + jnp.maximum(q, 0)]
        return jnp.where(jnp.logical_and(p >= 0, q >= 0), value, 0.0)

    for a in range(4):
        for b in range(2):
            give[BLK * a : BLK * a + BLK, BLK * b : BLK * b + BLK] = tile(from_rows[a], theirs[b])
    swap = remote(give, take, xs.at[2], xr.at[2], other)
    swap.start()

    swap.wait_recv()
    for a in range(4):
        for b in range(2):
            at = (slice(BLK * a, BLK * a + BLK), slice(BLK * b, BLK * b + BLK))
            asm[at] = root[at] + (tile(from_rows[a], ours[b]) + take[at])
    sc2[rows_of(row), :] = asm[0:PB, :]
    ring_start2()
    piece_wait2()
    unpack_pieces(pc2, rb2)
    block_start2(0)
    a2[rows_of(col), :] = rb2[...]
    own_columns = sr2.at[rows_of(col), :]
    copy_columns = remote(own_columns, own_columns, xs.at[3], xr.at[3], other)

    @pl.when(half == 0)
    def _():
        sr2[rows_of(col), :] = jnp.concatenate(
            [jnp.transpose(asm[BLK * i : BLK * i + BLK, 0:BLK])[0:PB] for i in range(4)], axis=1
        )
        copy_columns.start()

    relay2(1)
    relay2(2)

    def between2(i):
        for v in (1, 2, 3):

            @pl.when(i == v - 1)
            def _(v=v):
                block_start2(v)

        @pl.when(i == 3)
        def _():
            @pl.when(half == 1)
            def _():
                copy_columns.wait_recv()

            column_start2()

        relay2(i + 3)

    factor(a2, inv2, block_arrived2, between2)
    ring_end2()
    column_wait2()
    solve(a2, inv2, [(sc2, rp), (sr2, yr2)])
    for t in range(2):
        rpanel_ref[pl.ds(t, ORD, stride=2), :] = rp[:, BLK * t : BLK * t + BLK]
    for i in range(4):
        rows = slice(BLK * i, BLK * i + BLK)
        block = asm[rows, :] - dot_t(yr2[:, rows], rp[...])
        for t in range(2):
            out_ref[pl.ds(2 * BLK * i + t, BLK, stride=2), :] = block[:, BLK * t : BLK * t + BLK]

    @pl.when(half == 0)
    def _():
        copy_columns.wait_send()

    for copy in (root_corner, swap_corner, swap):
        copy.wait_send()
    for end in (piece_end, block_end, column_end, piece_end2, block_end2, column_end2):
        end()


def body(child_front, child_map, root_front):
    sds = jax.ShapeDtypeStruct
    full, side = (ORD, ORD), (ORD, ORD // 2)
    sems = [N, N, 4 * N, 4 * N] + [N] * 6 + [4, 4] + [N, N, 4 * N, 4 * N] + [N] * 6
    shapes = [
        (N, 8, BLK), (PB, ORD), full, (4, BLK, BLK), full, (ORD, 3 * BLK), (ORD, 3 * BLK), (9, BLK, BLK), side, side,
        (PB, BLK), (PB, BLK), (PB, BLK), (N, 8, BLK), (PB, ORD), full, (4, BLK, BLK), side, full, full, side, side, side,
    ]
    panel, root_panel, root_update = pl.pallas_call(
        kernel,
        out_shape=[sds(full, F32), sds((2 * ORD, BLK), F32), sds((2 * ORD, BLK), F32)],
        in_specs=[SM, VM, VM],
        out_specs=[VM, VM, VM],
        scratch_shapes=[*(pltpu.VMEM(s, F32) for s in shapes), *(pltpu.SemaphoreType.DMA((n,)) for n in sems)],
        compiler_params=pltpu.CompilerParams(
            collective_id=0, has_side_effects=True, vmem_limit_bytes=48 * 2**20
        ),
    )(child_map, child_front[0], root_front.reshape(2 * ORD, BLK))
    out = (ORD, 1, 1, ORD // 2)
    return (panel[None], root_panel.reshape(out), root_update.reshape(out))


def solution(mesh):
    return jax.shard_map(
        body,
        mesh=mesh,
        in_specs=(P("half", "row", "col"), P("half", None), P("row", "col", "half", None)),
        out_specs=(
            P("half", None, "col"),
            P(None, "col", "half", None),
            P("row", "col", "half", None),
        ),
        check_vma=False,
    )
```

```python
import jax
import jax.numpy as jnp
from jax import lax
from jax.experimental import pallas as pl
from jax.experimental.pallas import tpu as pltpu
from jax.sharding import PartitionSpec as P

N = 16
PB = 32
BLK = 128
ORD = N * PB
F32 = jnp.float32
MESH = pl.DeviceIdType.MESH
VM = pl.BlockSpec(memory_space=pltpu.VMEM)
SM = pl.BlockSpec(memory_space=pltpu.SMEM)


def dot(a, b):
    return lax.dot_general(
        a, b, (((1,), (0,)), ((), ())), precision=lax.Precision.HIGHEST, preferred_element_type=F32
    )


def dot_t(a, b):
    return lax.dot_general(
        a, b, (((0,), (0,)), ((), ())), precision=lax.Precision.HIGHEST, preferred_element_type=F32
    )


def factor_tile(a, at_half):
    n, full = BLK // 8, (8, BLK)
    diag = lax.broadcasted_iota(jnp.int32, (BLK, BLK), 0) == lax.broadcasted_iota(jnp.int32, (BLK, BLK), 1)
    only = jnp.where(diag, a, 0.0)
    scale = lax.rsqrt(jnp.sum(only, axis=0, keepdims=True))
    a = a * lax.rsqrt(jnp.sum(only, axis=1, keepdims=True)) * scale
    lane = lax.broadcasted_iota(jnp.int32, full, 1)
    sub = lax.broadcasted_iota(jnp.int32, full, 0)
    rows = [a[8 * i : 8 * i + 8] for i in range(n)]
    out = []
    for m in range(n):
        if m == n // 2:
            at_half()
        j0 = 8 * m
        left = lane < j0 + 8
        pivots = jnp.logical_and(lane >= j0, left)
        cols = [jnp.broadcast_to(rows[m][:, j0 + k : j0 + k + 1], full) for k in range(8)]
        e = {(i, k): jnp.broadcast_to(cols[k][i : i + 1], full) for k in range(8) for i in range(k, 8)}
        top = jnp.where(pivots, jnp.where(lane == sub + j0, 1.0, 0.0), rows[m])
        u = [jnp.broadcast_to(top[i : i + 1], full) for i in range(8)]
        r, low = [None] * 8, {}
        for k in range(0, 8, 2):
            pa, pb, pc = e[k, k], e[k + 1, k], e[k + 1, k + 1]
            r[k] = lax.rsqrt(pa)
            r[k + 1] = lax.rsqrt(pa * pc - pb * pb) * (pa * r[k])
            for i in range(k + 1, 8):
                low[i, k] = e[i, k] * r[k]
            for i in range(k + 2, 8):
                low[i, k + 1] = (e[i, k + 1] - low[i, k] * low[k + 1, k]) * r[k + 1]
            for i in range(k + 2, 8):
                for j in range(k + 2, i + 1):
                    e[i, j] = (e[i, j] - low[i, k] * low[j, k]) - low[i, k + 1] * low[j, k + 1]
            for p in (k, k + 1):
                u[p] = u[p] * r[p]
                for i in range(p + 1, 8):
                    u[i] = u[i] - low[i, p] * u[p]
        done = u[0]
        for k in range(1, 8):
            done = jnp.where(sub == k, u[k], done)
        out.append(jnp.where(left, done, 0.0))
        for q in range(m + 1, n):
            src = rows[q]
            t, lq = jnp.where(pivots, 0.0, src), []
            for k in range(8):
                v = jnp.broadcast_to(src[:, j0 + k : j0 + k + 1], full)
                for p in range(k):
                    v = v - lq[p] * low[k, p]
                v = v * r[k]
                lq.append(v)
                t = t - v * u[k]
            rows[q] = t
    return jnp.concatenate(out, axis=0) * scale


def factor(a_ref, i_ref, arrived, between):
    n = ORD // BLK

    def tiles(v):
        return slice(BLK * v, BLK * v + BLK)

    def turn(v):
        for i in range(v + 1, n):
            arrived(v, i)
        for i in range(v + 1, n):
            a_ref[tiles(v), tiles(i)] = jnp.transpose(a_ref[tiles(i), tiles(v)])

    def step(j, carry):
        jb = pl.multiple_of(j * BLK, BLK)
        arrived(j, j)
        for v in range(1, n):

            @pl.when(j == v)
            def _(v=v):
                turn(v)
                a_ref[tiles(v), BLK * v :] -= dot_t(a_ref[0 : BLK * v, tiles(v)], a_ref[0 : BLK * v, BLK * v :])

        between(2 * j)
        i_ref[j] = factor_tile(a_ref[pl.ds(jb, BLK), pl.ds(jb, BLK)], lambda: between(2 * j + 1))
        for v in range(n - 1):

            @pl.when(j == v)
            def _(v=v):
                if v == 0:
                    turn(v)
                here = (tiles(v), slice(BLK * v + BLK, ORD))
                a_ref[here] = dot(i_ref[v], a_ref[here])

        return carry

    lax.fori_loop(0, n, step, 0)


def solve(a_ref, i_ref, pairs):
    for j in range(ORD // BLK):
        here = slice(BLK * j, BLK * j + BLK)
        for s_ref, y_ref in pairs:
            acc = s_ref[here, :]
            if j:
                acc = acc - dot_t(a_ref[0 : BLK * j, here], y_ref[0 : BLK * j, :])
            y_ref[here, :] = dot(i_ref[j], acc)


def remote(src, dst, send_sem, recv_sem, dev):
    return pltpu.make_async_remote_copy(
        src_ref=src,
        dst_ref=dst,
        send_sem=send_sem,
        recv_sem=recv_sem,
        device_id=dev,
        device_id_type=MESH,
    )


def each(lo, hi, fn):
    def go(k, carry):
        fn(k)
        return carry

    lax.fori_loop(lo, hi, go, 0)


def rows_of(k):
    return pl.ds(pl.multiple_of(k * PB, PB), PB)


def ring(ref, row, sems):
    rs, rr, ls, lr = sems
    right, left = {"row": lax.rem(row + 1, N)}, {"row": lax.rem(row + N - 1, N)}
    wide = ref.shape[1] // 2

    def part(block, p):
        return ref.at[rows_of(block), wide * p : wide * p + wide]

    def to_right(s, p):
        view = part(lax.rem(row - s + N, N), p)
        return remote(view, view, rs.at[2 * s + p], rr.at[2 * s + p], right)

    def to_left(s, p):
        view = part(lax.rem(row + s, N), p)
        return remote(view, view, ls.at[2 * s + p], lr.at[2 * s + p], left)

    def got_right(s, p):
        view = part(lax.rem(row - 1 - s + 2 * N, N), p)
        return remote(view, view, rs.at[2 * s + p], rr.at[2 * s + p], right)

    def got_left(s, p):
        view = part(lax.rem(row + 1 + s, N), p)
        return remote(view, view, ls.at[2 * s + p], lr.at[2 * s + p], left)

    def start():
        for p in range(2):
            to_right(0, p).start()
            to_left(0, p).start()

    def relay(s):
        @pl.when(s < 7)
        def _():
            for p in range(2):
                got_right(s - 1, p).wait_recv()
                to_right(s, p).start()
                got_left(s - 1, p).wait_recv()
                to_left(s, p).start()

        @pl.when(s == 7)
        def _():
            for p in range(2):
                got_right(s - 1, p).wait_recv()
                to_right(s, p).start()

    def finish():
        for p in range(2):
            got_right(7, p).wait_recv()
            got_left(6, p).wait_recv()
        for p in range(2):
            each(0, 8, lambda s, p=p: to_right(s, p).wait_send())
            each(0, 7, lambda s, p=p: to_left(s, p).wait_send())

    return start, relay, finish


def packed_piece(tile):
    turned = jnp.transpose(tile)
    lane = lax.broadcasted_iota(jnp.int32, (8, BLK), 1)
    out = turned[0:8]
    for g in range(1, 4):
        out = jnp.where(lane >= PB * g, pltpu.roll(turned[8 * g : 8 * g + 8], PB * g, 1), out)
    return out


def unpack_pieces(pc_ref, rb_ref):
    lane = lax.broadcasted_iota(jnp.int32, (8, BLK), 1)
    for l in range(4):
        pcs = [pc_ref[4 * l + kk] for kk in range(4)]
        for g in range(4):
            out = None
            for kk in range(4):
                shift = (PB * (kk - g)) % BLK
                v = pltpu.roll(pcs[kk], shift, 1) if shift else pcs[kk]
                out = v if kk == 0 else jnp.where(lane >= PB * kk, v, out)
            rb_ref[8 * g : 8 * g + 8, BLK * l : BLK * l + BLK] = out


def greet(devices):
    barrier = pltpu.get_barrier_semaphore()
    for count, dev in devices:
        each(1, count + 1, lambda k, dev=dev: pl.semaphore_signal(barrier, inc=1, device_id=dev(k), device_id_type=MESH))
    return lambda: pl.semaphore_wait(barrier, sum(count for count, _ in devices))


def row_gather(pc, row, send, recv):
    def to(k):
        return remote(pc.at[row], pc.at[row], send.at[k], recv.at[row], {"row": lax.rem(row + k, N)})

    def got(k):
        view = pc.at[lax.rem(row + k, N)]
        return remote(view, view, send.at[k], recv.at[lax.rem(row + k, N)], {"row": row})

    def start():
        each(1, N, lambda k: to(k).start())

    def wait():
        each(1, N, lambda k: got(k).wait_recv())

    def finish():
        each(1, N, lambda k: to(k).wait_send())

    return start, wait, finish


def corner_gather(rb, a_ref, col, send, recv):
    group = col // 4

    def lanes(v):
        return pl.ds(pl.multiple_of(v * BLK, BLK), BLK)

    def to(k, v):
        dst = a_ref.at[rows_of(col), lanes(v)]
        return remote(
            rb.at[:, lanes(v)], dst, send.at[v * N + k], recv.at[v * N + col], {"col": lax.rem(col + k, N)}
        )

    def start(v):
        @pl.when(group >= v)
        def _():
            each(1, N, lambda k: to(k, v).start())

    def arrived(v, g):
        def one(i):
            src = 4 * g + i

            @pl.when(src != col)
            def _():
                view = a_ref.at[rows_of(src), lanes(v)]
                remote(view, view, send.at[0], recv.at[v * N + src], {"col": src}).wait_recv()

        each(0, 4, one)

    def finish():
        for v in range(4):

            @pl.when(group >= v)
            def _(v=v):
                each(1, N, lambda k: to(k, v).wait_send())

    return start, arrived, finish


def column_gather(sr, col, send, recv):
    def to(k):
        view = sr.at[rows_of(col), :]
        return remote(view, view, send.at[k], recv.at[col], {"col": lax.rem(col + k, N)})

    def got(k):
        src = lax.rem(col + k, N)
        view = sr.at[rows_of(src), :]
        return remote(view, view, send.at[k], recv.at[src], {"col": col})

    def start():
        each(1, N, lambda k: to(k).start())

    def wait():
        each(1, N, lambda k: got(k).wait_recv())

    def finish():
        each(1, N, lambda k: to(k).wait_send())

    return start, wait, finish


def split_sides(src, dst):
    for t in range(2):
        dst[:, BLK * t : BLK * t + BLK] = src[pl.ds(t, ORD, stride=2), :]


def kernel(
    map_ref, blk_ref, root_ref, panel_ref, rpanel_ref, out_ref,
    pc, rb, a_ref, inv_ref, sc, sr, yr, upd, give, take, rx, cg, ct,
    pc2, rb2, a2, inv2, sc2, sr2, yr2, asm, root, rp, cs, cy,
    s1, r1, s2, r2, s4, r4, rs, rr, ls, lr, xs, xr,
    s5, r5, s6, r6, s8, r8, rs2, rr2, ls2, lr2,
):
    half, row, col = lax.axis_index("half"), lax.axis_index("row"), lax.axis_index("col")
    other = {"half": 1 - half}
    piece_start, piece_wait, piece_end = row_gather(pc, row, s1, r1)
    block_start, block_arrived, block_end = corner_gather(rb, a_ref, col, s2, r2)
    column_start, column_wait, column_end = column_gather(sr, col, s4, r4)
    ring_start, relay, ring_end = ring(sc, row, (rs, rr, ls, lr))
    piece_start2, piece_wait2, piece_end2 = row_gather(pc2, row, s5, r5)
    block_start2, block_arrived2, block_end2 = corner_gather(rb2, a2, col, s6, r6)
    column_start2, column_wait2, column_end2 = column_gather(sr2, col, s8, r8)
    ring_start2, relay2, ring_end2 = ring(sc2, row, (rs2, rr2, ls2, lr2))

    wait_all = greet(
        [
            (N - 1, lambda k: {"row": lax.rem(row + k, N)}),
            (N - 1, lambda k: {"col": lax.rem(col + k, N)}),
            (1, lambda k: other),
        ]
    )
    pc[row] = packed_piece(blk_ref[0:BLK, 0:BLK])
    sc[rows_of(row), :] = blk_ref[0:PB, :]
    sr[rows_of(col), :] = jnp.concatenate(
        [jnp.transpose(blk_ref[BLK * i : BLK * i + BLK, 0:BLK])[0:PB] for i in range(1, 4)], axis=1
    )
    split_sides(root_ref, root)
    wait_all()
    piece_start()
    ring_start()
    root_corner = remote(root.at[0:PB, 0:BLK], rx, xs.at[0], xr.at[0], other)
    root_corner.start()
    relay(1)
    piece_wait()
    unpack_pieces(pc, rb)
    block_start(0)
    a_ref[rows_of(col), :] = rb[...]
    relay(2)
    relay(3)

    def between(i):
        for v in (1, 2, 3):

            @pl.when(i == v - 1)
            def _(v=v):
                block_start(v)

        @pl.when(i == 2)
        def _():
            column_start()

        relay(i + 4)

    factor(a_ref, inv_ref, block_arrived, between)
    ring_end()
    column_wait()

    def source(part, target):
        found = jnp.int32(-1)
        for u in range(3):
            found = jnp.where(map_ref[0, 3 * part + u] == 4 * part + target, jnp.int32(u), found)
        return found

    from_rows = [source(row, a) for a in range(4)]
    theirs = [source(col, 2 * (1 - half) + b) for b in range(2)]
    ours = [source(col, 2 * half + b) for b in range(2)]
    p, q = from_rows[0], source(col, 0)
    inside = jnp.logical_and(p >= 0, q >= 0)

    def pick(which, get):
        return jnp.where(which == 2, get(2), jnp.where(which == 1, get(1), get(0)))

    def lanes(v):
        return slice(BLK + BLK * v, 2 * BLK + BLK * v)

    cs[:, 0:BLK] = pick(q, lambda v: sc[:, lanes(v)])
    cs[:, BLK:] = pick(p, lambda u: sr[:, BLK * u : BLK * u + BLK])
    solve(a_ref, inv_ref, [(cs, cy)])
    corner = pick(p, lambda u: pick(q, lambda v: blk_ref[BLK + BLK * u : BLK + BLK * u + PB, lanes(v)]))
    corner = corner - dot_t(cy[:, BLK:], cy[:, 0:BLK])[0:PB]
    cg[...] = jnp.where(inside, corner, 0.0)
    swap_corner = remote(cg, ct, xs.at[1], xr.at[1], other)
    swap_corner.start()
    solve(a_ref, inv_ref, [(sr, yr)])
    root_corner.wait_recv()
    base = jnp.where(half == 0, root[0:PB, 0:BLK], rx[...])
    swap_corner.wait_recv()
    corner = base + (cg[...] + ct[...])
    pc2[row] = packed_piece(jnp.concatenate([corner] * 4, axis=0))
    piece_start2()
    solve(a_ref, inv_ref, [(sc, panel_ref)])
    for u in range(3):
        rows = slice(BLK * u, BLK * u + BLK)
        block = blk_ref[BLK + BLK * u : 2 * BLK + BLK * u, BLK:] - dot_t(yr[:, rows], panel_ref[:, BLK:])
        for v in range(3):
            upd[3 * u + v] = block[:, BLK * v : BLK * v + BLK]

    def tile(p, q):
        value = upd[jnp.maximum(p, 0) * 3 + jnp.maximum(q, 0)]
        return jnp.where(jnp.logical_and(p >= 0, q >= 0), value, 0.0)

    for a in range(4):
        for b in range(2):
            give[BLK * a : BLK * a + BLK, BLK * b : BLK * b + BLK] = tile(from_rows[a], theirs[b])
    swap = remote(give, take, xs.at[2], xr.at[2], other)
    swap.start()

    piece_wait2()
    unpack_pieces(pc2, rb2)
    block_start2(0)
    a2[rows_of(col), :] = rb2[...]
    swap.wait_recv()
    for a in range(4):
        for b in range(2):
            at = (slice(BLK * a, BLK * a + BLK), slice(BLK * b, BLK * b + BLK))
            asm[at] = root[at] + (tile(from_rows[a], ours[b]) + take[at])
    sc2[rows_of(row), :] = asm[0:PB, :]
    ring_start2()
    own_columns = sr2.at[rows_of(col), :]
    copy_columns = remote(own_columns, own_columns, xs.at[3], xr.at[3], other)

    @pl.when(half == 0)
    def _():
        sr2[rows_of(col), :] = jnp.concatenate(
            [jnp.transpose(asm[BLK * i : BLK * i + BLK, 0:BLK])[0:PB] for i in range(4)], axis=1
        )
        copy_columns.start()

    relay2(1)
    relay2(2)

    def between2(i):
        for v in (1, 2, 3):

            @pl.when(i == v - 1)
            def _(v=v):
                block_start2(v)

        @pl.when(i == 2)
        def _():
            @pl.when(half == 1)
            def _():
                copy_columns.wait_recv()

            column_start2()

        relay2(i + 3)

    factor(a2, inv2, block_arrived2, between2)
    ring_end2()
    column_wait2()
    solve(a2, inv2, [(sc2, rp), (sr2, yr2)])
    for t in range(2):
        rpanel_ref[pl.ds(t, ORD, stride=2), :] = rp[:, BLK * t : BLK * t + BLK]
    for i in range(4):
        rows = slice(BLK * i, BLK * i + BLK)
        block = asm[rows, :] - dot_t(yr2[:, rows], rp[...])
        for t in range(2):
            out_ref[pl.ds(2 * BLK * i + t, BLK, stride=2), :] = block[:, BLK * t : BLK * t + BLK]

    @pl.when(half == 0)
    def _():
        copy_columns.wait_send()

    for copy in (root_corner, swap_corner, swap):
        copy.wait_send()
    for end in (piece_end, block_end, column_end, piece_end2, block_end2, column_end2):
        end()


def body(child_front, child_map, root_front):
    sds = jax.ShapeDtypeStruct
    full, side = (ORD, ORD), (ORD, ORD // 2)
    sems = [N, N, 4 * N, 4 * N] + [N] * 6 + [4, 4] + [N, N, 4 * N, 4 * N] + [N] * 6
    shapes = [
        (N, 8, BLK), (PB, ORD), full, (4, BLK, BLK), full, (ORD, 3 * BLK), (ORD, 3 * BLK), (9, BLK, BLK), side, side,
        (PB, BLK), (PB, BLK), (PB, BLK), (N, 8, BLK), (PB, ORD), full, (4, BLK, BLK), side, full, full, side, side, side,
        side, side,
    ]
    panel, root_panel, root_update = pl.pallas_call(
        kernel,
        out_shape=[sds(full, F32), sds((2 * ORD, BLK), F32), sds((2 * ORD, BLK), F32)],
        in_specs=[SM, VM, VM],
        out_specs=[VM, VM, VM],
        scratch_shapes=[*(pltpu.VMEM(s, F32) for s in shapes), *(pltpu.SemaphoreType.DMA((n,)) for n in sems)],
        compiler_params=pltpu.CompilerParams(
            collective_id=0, has_side_effects=True, vmem_limit_bytes=48 * 2**20
        ),
    )(child_map, child_front[0], root_front.reshape(2 * ORD, BLK))
    out = (ORD, 1, 1, ORD // 2)
    return (panel[None], root_panel.reshape(out), root_update.reshape(out))


def solution(mesh):
    return jax.shard_map(
        body,
        mesh=mesh,
        in_specs=(P("half", "row", "col"), P("half", None), P("row", "col", "half", None)),
        out_specs=(
            P("half", None, "col"),
            P(None, "col", "half", None),
            P("row", "col", "half", None),
        ),
        check_vma=False,
    )
```

```python
import jax
import jax.numpy as jnp
from jax import lax
from jax.experimental import pallas as pl
from jax.experimental.pallas import tpu as pltpu
from jax.sharding import PartitionSpec as P

N = 16
PB = 32
BLK = 128
ORD = N * PB
F32 = jnp.float32
MESH = pl.DeviceIdType.MESH
VM = pl.BlockSpec(memory_space=pltpu.VMEM)
SM = pl.BlockSpec(memory_space=pltpu.SMEM)


def dot(a, b):
    return lax.dot_general(
        a, b, (((1,), (0,)), ((), ())), precision=lax.Precision.HIGHEST, preferred_element_type=F32
    )


def dot_t(a, b):
    return lax.dot_general(
        a, b, (((0,), (0,)), ((), ())), precision=lax.Precision.HIGHEST, preferred_element_type=F32
    )


def factor_tile(a, at_half):
    n, full = BLK // 8, (8, BLK)
    diag = lax.broadcasted_iota(jnp.int32, (BLK, BLK), 0) == lax.broadcasted_iota(jnp.int32, (BLK, BLK), 1)
    only = jnp.where(diag, a, 0.0)
    scale = lax.rsqrt(jnp.sum(only, axis=0, keepdims=True))
    a = a * lax.rsqrt(jnp.sum(only, axis=1, keepdims=True)) * scale
    lane = lax.broadcasted_iota(jnp.int32, full, 1)
    sub = lax.broadcasted_iota(jnp.int32, full, 0)
    rows = [a[8 * i : 8 * i + 8] for i in range(n)]
    out = []
    for m in range(n):
        if m == n // 2:
            at_half()
        j0 = 8 * m
        left = lane < j0 + 8
        pivots = jnp.logical_and(lane >= j0, left)
        cols = [jnp.broadcast_to(rows[m][:, j0 + k : j0 + k + 1], full) for k in range(8)]
        e = {(i, k): jnp.broadcast_to(cols[k][i : i + 1], full) for k in range(8) for i in range(k, 8)}
        top = jnp.where(pivots, jnp.where(lane == sub + j0, 1.0, 0.0), rows[m])
        u = [jnp.broadcast_to(top[i : i + 1], full) for i in range(8)]
        r, low = [None] * 8, {}
        for k in range(0, 8, 2):
            pa, pb, pc = e[k, k], e[k + 1, k], e[k + 1, k + 1]
            r[k] = lax.rsqrt(pa)
            r[k + 1] = lax.rsqrt(pa * pc - pb * pb) * (pa * r[k])
            for i in range(k + 1, 8):
                low[i, k] = e[i, k] * r[k]
            for i in range(k + 2, 8):
                low[i, k + 1] = (e[i, k + 1] - low[i, k] * low[k + 1, k]) * r[k + 1]
            for i in range(k + 2, 8):
                for j in range(k + 2, i + 1):
                    e[i, j] = (e[i, j] - low[i, k] * low[j, k]) - low[i, k + 1] * low[j, k + 1]
            for p in (k, k + 1):
                u[p] = u[p] * r[p]
                for i in range(p + 1, 8):
                    u[i] = u[i] - low[i, p] * u[p]
        done = u[0]
        for k in range(1, 8):
            done = jnp.where(sub == k, u[k], done)
        out.append(jnp.where(left, done, 0.0))
        for q in range(m + 1, n):
            src = rows[q]
            t, lq = jnp.where(pivots, 0.0, src), []
            for k in range(8):
                v = jnp.broadcast_to(src[:, j0 + k : j0 + k + 1], full)
                for p in range(k):
                    v = v - lq[p] * low[k, p]
                v = v * r[k]
                lq.append(v)
                t = t - v * u[k]
            rows[q] = t
    return jnp.concatenate(out, axis=0) * scale


def factor(a_ref, i_ref, arrived, between):
    n = ORD // BLK

    def tiles(v):
        return slice(BLK * v, BLK * v + BLK)

    def turn(v):
        for i in range(v + 1, n):
            arrived(v, i)
        for i in range(v + 1, n):
            a_ref[tiles(v), tiles(i)] = jnp.transpose(a_ref[tiles(i), tiles(v)])

    def step(j, carry):
        jb = pl.multiple_of(j * BLK, BLK)
        arrived(j, j)
        for v in range(1, n):

            @pl.when(j == v)
            def _(v=v):
                turn(v)
                a_ref[tiles(v), BLK * v :] -= dot_t(a_ref[0 : BLK * v, tiles(v)], a_ref[0 : BLK * v, BLK * v :])

        between(2 * j)
        i_ref[j] = factor_tile(a_ref[pl.ds(jb, BLK), pl.ds(jb, BLK)], lambda: between(2 * j + 1))
        for v in range(n - 1):

            @pl.when(j == v)
            def _(v=v):
                if v == 0:
                    turn(v)
                here = (tiles(v), slice(BLK * v + BLK, ORD))
                a_ref[here] = dot(i_ref[v], a_ref[here])

        return carry

    lax.fori_loop(0, n, step, 0)


def solve(a_ref, i_ref, pairs):
    for j in range(ORD // BLK):
        here = slice(BLK * j, BLK * j + BLK)
        for s_ref, y_ref in pairs:
            acc = s_ref[here, :]
            if j:
                acc = acc - dot_t(a_ref[0 : BLK * j, here], y_ref[0 : BLK * j, :])
            y_ref[here, :] = dot(i_ref[j], acc)


def remote(src, dst, send_sem, recv_sem, dev):
    return pltpu.make_async_remote_copy(
        src_ref=src,
        dst_ref=dst,
        send_sem=send_sem,
        recv_sem=recv_sem,
        device_id=dev,
        device_id_type=MESH,
    )


def each(lo, hi, fn):
    def go(k, carry):
        fn(k)
        return carry

    lax.fori_loop(lo, hi, go, 0)


def rows_of(k):
    return pl.ds(pl.multiple_of(k * PB, PB), PB)


def ring(ref, row, sems):
    rs, rr, ls, lr = sems
    right, left = {"row": lax.rem(row + 1, N)}, {"row": lax.rem(row + N - 1, N)}
    wide = ref.shape[1] // 2

    def part(block, p):
        return ref.at[rows_of(block), wide * p : wide * p + wide]

    def to_right(s, p):
        view = part(lax.rem(row - s + N, N), p)
        return remote(view, view, rs.at[2 * s + p], rr.at[2 * s + p], right)

    def to_left(s, p):
        view = part(lax.rem(row + s, N), p)
        return remote(view, view, ls.at[2 * s + p], lr.at[2 * s + p], left)

    def got_right(s, p):
        view = part(lax.rem(row - 1 - s + 2 * N, N), p)
        return remote(view, view, rs.at[2 * s + p], rr.at[2 * s + p], right)

    def got_left(s, p):
        view = part(lax.rem(row + 1 + s, N), p)
        return remote(view, view, ls.at[2 * s + p], lr.at[2 * s + p], left)

    def start():
        for p in range(2):
            to_right(0, p).start()
            to_left(0, p).start()

    def relay(s):
        @pl.when(s < 7)
        def _():
            for p in range(2):
                got_right(s - 1, p).wait_recv()
                to_right(s, p).start()
                got_left(s - 1, p).wait_recv()
                to_left(s, p).start()

        @pl.when(s == 7)
        def _():
            for p in range(2):
                got_right(s - 1, p).wait_recv()
                to_right(s, p).start()

    def finish():
        for p in range(2):
            got_right(7, p).wait_recv()
            got_left(6, p).wait_recv()
        for p in range(2):
            each(0, 8, lambda s, p=p: to_right(s, p).wait_send())
            each(0, 7, lambda s, p=p: to_left(s, p).wait_send())

    return start, relay, finish


def packed_piece(tile):
    turned = jnp.transpose(tile)
    lane = lax.broadcasted_iota(jnp.int32, (8, BLK), 1)
    out = turned[0:8]
    for g in range(1, 4):
        out = jnp.where(lane >= PB * g, pltpu.roll(turned[8 * g : 8 * g + 8], PB * g, 1), out)
    return out


def unpack_pieces(pc_ref, rb_ref):
    lane = lax.broadcasted_iota(jnp.int32, (8, BLK), 1)
    for l in range(4):
        pcs = [pc_ref[4 * l + kk] for kk in range(4)]
        for g in range(4):
            out = None
            for kk in range(4):
                shift = (PB * (kk - g)) % BLK
                v = pltpu.roll(pcs[kk], shift, 1) if shift else pcs[kk]
                out = v if kk == 0 else jnp.where(lane >= PB * kk, v, out)
            rb_ref[8 * g : 8 * g + 8, BLK * l : BLK * l + BLK] = out


def greet(devices):
    barrier = pltpu.get_barrier_semaphore()
    for count, dev in devices:
        each(1, count + 1, lambda k, dev=dev: pl.semaphore_signal(barrier, inc=1, device_id=dev(k), device_id_type=MESH))
    return lambda: pl.semaphore_wait(barrier, sum(count for count, _ in devices))


def row_gather(pc, row, send, recv):
    def to(k):
        return remote(pc.at[row], pc.at[row], send.at[k], recv.at[row], {"row": lax.rem(row + k, N)})

    def got(k):
        view = pc.at[lax.rem(row + k, N)]
        return remote(view, view, send.at[k], recv.at[lax.rem(row + k, N)], {"row": row})

    def start():
        each(1, N, lambda k: to(k).start())

    def wait():
        each(1, N, lambda k: got(k).wait_recv())

    def finish():
        each(1, N, lambda k: to(k).wait_send())

    return start, wait, finish


def corner_gather(rb, a_ref, col, send, recv):
    group = col // 4

    def lanes(v):
        return pl.ds(pl.multiple_of(v * BLK, BLK), BLK)

    def to(k, v):
        dst = a_ref.at[rows_of(col), lanes(v)]
        return remote(
            rb.at[:, lanes(v)], dst, send.at[v * N + k], recv.at[v * N + col], {"col": lax.rem(col + k, N)}
        )

    def start(v):
        @pl.when(group >= v)
        def _():
            each(1, N, lambda k: to(k, v).start())

    def arrived(v, g):
        def one(i):
            src = 4 * g + i

            @pl.when(src != col)
            def _():
                view = a_ref.at[rows_of(src), lanes(v)]
                remote(view, view, send.at[0], recv.at[v * N + src], {"col": src}).wait_recv()

        each(0, 4, one)

    def finish():
        for v in range(4):

            @pl.when(group >= v)
            def _(v=v):
                each(1, N, lambda k: to(k, v).wait_send())

    return start, arrived, finish


def column_gather(sr, col, send, recv):
    def to(k):
        view = sr.at[rows_of(col), :]
        return remote(view, view, send.at[k], recv.at[col], {"col": lax.rem(col + k, N)})

    def got(k):
        src = lax.rem(col + k, N)
        view = sr.at[rows_of(src), :]
        return remote(view, view, send.at[k], recv.at[src], {"col": col})

    def start():
        each(1, N, lambda k: to(k).start())

    def wait():
        each(1, N, lambda k: got(k).wait_recv())

    def finish():
        each(1, N, lambda k: to(k).wait_send())

    return start, wait, finish


def split_sides(src, dst):
    for t in range(2):
        dst[:, BLK * t : BLK * t + BLK] = src[pl.ds(t, ORD, stride=2), :]


def kernel(
    map_ref, blk_ref, root_ref, panel_ref, rpanel_ref, out_ref,
    pc, rb, a_ref, inv_ref, sc, sr, yr, upd, give, take, rx, cg, ct,
    pc2, rb2, a2, inv2, sc2, sr2, yr2, asm, root, rp,
    s1, r1, s2, r2, s4, r4, rs, rr, ls, lr, xs, xr,
    s5, r5, s6, r6, s8, r8, rs2, rr2, ls2, lr2,
):
    half, row, col = lax.axis_index("half"), lax.axis_index("row"), lax.axis_index("col")
    other = {"half": 1 - half}
    piece_start, piece_wait, piece_end = row_gather(pc, row, s1, r1)
    block_start, block_arrived, block_end = corner_gather(rb, a_ref, col, s2, r2)
    column_start, column_wait, column_end = column_gather(sr, col, s4, r4)
    ring_start, relay, ring_end = ring(sc, row, (rs, rr, ls, lr))
    piece_start2, piece_wait2, piece_end2 = row_gather(pc2, row, s5, r5)
    block_start2, block_arrived2, block_end2 = corner_gather(rb2, a2, col, s6, r6)
    column_start2, column_wait2, column_end2 = column_gather(sr2, col, s8, r8)
    ring_start2, relay2, ring_end2 = ring(sc2, row, (rs2, rr2, ls2, lr2))

    wait_all = greet(
        [
            (N - 1, lambda k: {"row": lax.rem(row + k, N)}),
            (N - 1, lambda k: {"col": lax.rem(col + k, N)}),
            (1, lambda k: other),
        ]
    )
    pc[row] = packed_piece(blk_ref[0:BLK, 0:BLK])
    sc[rows_of(row), :] = blk_ref[0:PB, :]
    sr[rows_of(col), :] = jnp.concatenate(
        [jnp.transpose(blk_ref[BLK * i : BLK * i + BLK, 0:BLK])[0:PB] for i in range(1, 4)], axis=1
    )
    split_sides(root_ref, root)
    wait_all()
    piece_start()
    ring_start()
    root_corner = remote(root.at[0:PB, 0:BLK], rx, xs.at[0], xr.at[0], other)
    root_corner.start()
    relay(1)
    piece_wait()
    unpack_pieces(pc, rb)
    block_start(0)
    a_ref[rows_of(col), :] = rb[...]
    relay(2)
    relay(3)

    def between(i):
        for v in (1, 2, 3):

            @pl.when(i == v - 1)
            def _(v=v):
                block_start(v)

        @pl.when(i == 3)
        def _():
            column_start()

        relay(i + 4)

    factor(a_ref, inv_ref, block_arrived, between)
    ring_end()
    column_wait()
    solve(a_ref, inv_ref, [(sc, panel_ref), (sr, yr)])

    def source(part, target):
        found = jnp.int32(-1)
        for u in range(3):
            found = jnp.where(map_ref[0, 3 * part + u] == 4 * part + target, jnp.int32(u), found)
        return found

    from_rows = [source(row, a) for a in range(4)]
    theirs = [source(col, 2 * (1 - half) + b) for b in range(2)]
    ours = [source(col, 2 * half + b) for b in range(2)]
    p = from_rows[0]

    def pick(which, get):
        return jnp.where(which == 2, get(2), jnp.where(which == 1, get(1), get(0)))

    strip = pick(p, lambda u: blk_ref[BLK + BLK * u : BLK + BLK * u + PB, BLK:]) - dot_t(
        pick(p, lambda u: yr[:, BLK * u : BLK * u + BLK]), panel_ref[:, BLK:]
    )[0:PB]
    for b in range(4):
        q = source(col, b)
        part = pick(q, lambda v: strip[:, BLK * v : BLK * v + BLK])
        cg[:, BLK * b : BLK * b + BLK] = jnp.where(jnp.logical_and(p >= 0, q >= 0), part, 0.0)
    swap_corner = remote(cg, ct, xs.at[1], xr.at[1], other)
    swap_corner.start()
    root_corner.wait_recv()
    base = jnp.where(half == 0, root[0:PB, 0:BLK], rx[...])
    swap_corner.wait_recv()
    corner = base + (cg[:, 0:BLK] + ct[:, 0:BLK])
    pc2[row] = packed_piece(jnp.concatenate([corner] * 4, axis=0))
    piece_start2()
    joined = cg[...] + ct[...]
    sc2[rows_of(row), :] = root[0:PB, :] + jnp.where(half == 0, joined[:, 0 : 2 * BLK], joined[:, 2 * BLK :])
    ring_start2()
    for u in range(3):
        rows = slice(BLK * u, BLK * u + BLK)
        block = blk_ref[BLK + BLK * u : 2 * BLK + BLK * u, BLK:] - dot_t(yr[:, rows], panel_ref[:, BLK:])
        for v in range(3):
            upd[3 * u + v] = block[:, BLK * v : BLK * v + BLK]

    def tile(p, q):
        value = upd[jnp.maximum(p, 0) * 3 + jnp.maximum(q, 0)]
        return jnp.where(jnp.logical_and(p >= 0, q >= 0), value, 0.0)

    for a in range(4):
        for b in range(2):
            give[BLK * a : BLK * a + BLK, BLK * b : BLK * b + BLK] = tile(from_rows[a], theirs[b])
    swap = remote(give, take, xs.at[2], xr.at[2], other)
    swap.start()

    relay2(1)
    swap.wait_recv()
    for a in range(4):
        for b in range(2):
            at = (slice(BLK * a, BLK * a + BLK), slice(BLK * b, BLK * b + BLK))
            asm[at] = root[at] + (tile(from_rows[a], ours[b]) + take[at])
    relay2(2)
    piece_wait2()
    unpack_pieces(pc2, rb2)
    block_start2(0)
    a2[rows_of(col), :] = rb2[...]
    own_columns = sr2.at[rows_of(col), :]
    copy_columns = remote(own_columns, own_columns, xs.at[3], xr.at[3], other)

    @pl.when(half == 0)
    def _():
        sr2[rows_of(col), :] = jnp.concatenate(
            [jnp.transpose(asm[BLK * i : BLK * i + BLK, 0:BLK])[0:PB] for i in range(4)], axis=1
        )
        copy_columns.start()

    relay2(3)

    def between2(i):
        for v in (1, 2, 3):

            @pl.when(i == v - 1)
            def _(v=v):
                block_start2(v)

        @pl.when(i == 2)
        def _():
            @pl.when(half == 1)
            def _():
                copy_columns.wait_recv()

            column_start2()

        relay2(i + 4)

    factor(a2, inv2, block_arrived2, between2)
    ring_end2()
    column_wait2()
    solve(a2, inv2, [(sc2, rp), (sr2, yr2)])
    for t in range(2):
        rpanel_ref[pl.ds(t, ORD, stride=2), :] = rp[:, BLK * t : BLK * t + BLK]
    for i in range(4):
        rows = slice(BLK * i, BLK * i + BLK)
        block = asm[rows, :] - dot_t(yr2[:, rows], rp[...])
        for t in range(2):
            out_ref[pl.ds(2 * BLK * i + t, BLK, stride=2), :] = block[:, BLK * t : BLK * t + BLK]

    @pl.when(half == 0)
    def _():
        copy_columns.wait_send()

    for copy in (root_corner, swap_corner, swap):
        copy.wait_send()
    for end in (piece_end, block_end, column_end, piece_end2, block_end2, column_end2):
        end()


def body(child_front, child_map, root_front):
    sds = jax.ShapeDtypeStruct
    full, side = (ORD, ORD), (ORD, ORD // 2)
    sems = [N, N, 4 * N, 4 * N] + [N] * 6 + [4, 4] + [N, N, 4 * N, 4 * N] + [N] * 6
    shapes = [
        (N, 8, BLK), (PB, ORD), full, (4, BLK, BLK), full, (ORD, 3 * BLK), (ORD, 3 * BLK), (9, BLK, BLK), side, side,
        (PB, BLK), (PB, ORD), (PB, ORD), (N, 8, BLK), (PB, ORD), full, (4, BLK, BLK), side, full, full, side, side, side,
    ]
    panel, root_panel, root_update = pl.pallas_call(
        kernel,
        out_shape=[sds(full, F32), sds((2 * ORD, BLK), F32), sds((2 * ORD, BLK), F32)],
        in_specs=[SM, VM, VM],
        out_specs=[VM, VM, VM],
        scratch_shapes=[*(pltpu.VMEM(s, F32) for s in shapes), *(pltpu.SemaphoreType.DMA((n,)) for n in sems)],
        compiler_params=pltpu.CompilerParams(
            collective_id=0, has_side_effects=True, vmem_limit_bytes=48 * 2**20
        ),
    )(child_map, child_front[0], root_front.reshape(2 * ORD, BLK))
    out = (ORD, 1, 1, ORD // 2)
    return (panel[None], root_panel.reshape(out), root_update.reshape(out))


def solution(mesh):
    return jax.shard_map(
        body,
        mesh=mesh,
        in_specs=(P("half", "row", "col"), P("half", None), P("row", "col", "half", None)),
        out_specs=(
            P("half", None, "col"),
            P(None, "col", "half", None),
            P("row", "col", "half", None),
        ),
        check_vma=False,
    )
```
